128 devices in a mesh: step: 8 (over z, x_hi), tok: 16 (over y, x_lo, core).
Axes of the slice: x: 4 (x_hi: 2, x_lo: 2; x = x_hi * 2 + x_lo), y: 4, z: 4, core: 2. Of those that a mesh axis runs over, the one named last changes fastest.
Arguments:
- latents: bfloat16 [8, 8192, 1152], P('step', 'tok'), may hold values from -6 to 6
- timesteps: int32 [32], replicated, may hold values from 0 to 63
- experts: int32 [32], replicated, may hold values from 0 to 1
- offset: int32 [1], replicated, may hold values from 0 to 24
- modulation: float32 [64, 3, 1152], replicated, may hold values from -4 to 4
- coef: float32 [64], replicated, may hold values from 0.1 to 1
- w_qkv: bfloat16 [2, 1152, 16, 216], P(None, None, 'tok'), may hold values from -1 to 1
- w_o: bfloat16 [2, 1152, 1152], P(None, 'tok'), may hold values from -0.1875 to 0.1875
- w_cq: bfloat16 [2, 1152, 1152], P(None, None, 'tok'), may hold values from -0.1875 to 0.1875
- w_co: bfloat16 [2, 1152, 1152], P(None, 'tok'), may hold values from -0.1875 to 0.1875
- text_kv: bfloat16 [2, 2, 300, 1152], replicated, may hold values from -240 to 240
Outputs:
- new_latents: bfloat16 [8, 8192, 1152], P('step', 'tok')
The draws below stay inside these ranges and needn't reach their ends.
All inputs are finite; a program needn't handle non-finite values.
Results may differ from the reference program's by a relative error of at most 0.028.
The reference program's roundings to bfloat16 on the way count: a program that leaves them out, or rounds other values in their place, can miss the bound.
Values may be sent and summed in bfloat16 or wider, within the bound.
No kernel may reach another device: no remote copies, remote signals or barrier semaphores. Data moves between devices by JAX's collectives and lax.ppermute only.
A program may use at most 128 MiB of HBM per device.

```python
import math
import jax
import jax.numpy as jnp
from jax import lax

D = 1152
HEADS = 16
HD = 72
TEXT = 300
NT = 64
SCHED = 32
STEPS = 8
TOKENS = 8192


def head_levels(key, strengths):
    levels_table = jnp.asarray(strengths, jnp.float32)

    def one_expert(expert_key):
        head_order = jax.random.permutation(expert_key, HEADS)
        return jnp.ones((HEADS,), jnp.float32).at[head_order[:levels_table.shape[0]]].set(levels_table)
    return jax.vmap(one_expert)(jax.random.split(key, 2))


def draw_w_qkv(key, part):
    key = jax.random.fold_in(key, 11)
    level_key, entry_key = jax.random.split(key)
    levels = head_levels(level_key, (2.4, 2.9, 3.4, 3.9))
    full_shape = (2, D, HEADS, 3 * HD)
    entries = jax.random.truncated_normal(entry_key, -4.0, 4.0, full_shape, jnp.float32)
    column = jnp.arange(3 * HD)
    boosted = jnp.where(column[None, None, :] < 2 * HD, levels[:, :, None], 1.0)
    weight = entries * boosted[:, None, :, :] * (D // 2) ** (-0.5)
    return jnp.clip(weight, -1.0, 1.0).astype(jnp.bfloat16)


def draw_text_kv(key, part):
    key = jax.random.fold_in(key, 23)
    level_key, entry_key = jax.random.split(key)
    levels = head_levels(level_key, (24.0, 36.0, 48.0, 60.0))
    full_shape = (2, 2, TEXT, HEADS, HD)
    entries = jax.random.truncated_normal(entry_key, -4.0, 4.0, full_shape, jnp.float32)
    kinds = jnp.arange(2)
    boosted = jnp.where(kinds[None, :, None, None, None] == 0, levels[:, None, None, :, None], 1.0)
    return (entries * boosted).reshape(2, 2, TEXT, HEADS * HD).astype(jnp.bfloat16)


def set_ends(values, own_key, smallest, largest):
    index_at = [jax.random.randint(jax.random.fold_in(own_key, axis), (), 0, length) for axis, length in enumerate(values.shape)]
    longest = values.shape.index(max(values.shape))
    neighbour = index_at[:longest] + [(index_at[longest] + 1) % values.shape[longest]] + index_at[longest + 1:]
    return values.at[tuple(index_at)].set(smallest).at[tuple(neighbour)].set(largest)


def shard_levels(rng, dims, cuts, least, high):
    def one(dim, blocks):
        steps = jax.random.uniform(jax.random.fold_in(jax.random.fold_in(rng, 6), dim), (blocks,), jnp.float32, least / len(cuts), high / len(cuts))
        return jnp.repeat(jnp.exp(steps), dims[dim] // blocks).reshape((-1,) + (1,) * (len(dims) - dim - 1))

    loudness = one(*cuts[0])
    for cut in cuts[1:]:
        loudness = loudness * one(*cut)
    return loudness


def gaussian(stream_key, dims, deviation, bound, cuts=(), kind=jnp.bfloat16):
    loudness = shard_levels(stream_key, dims, cuts, -0.22, 0.18) if cuts else 1.0
    values = jax.random.normal(stream_key, dims, jnp.float32) * deviation * loudness
    return jnp.minimum(jnp.maximum(values, -bound), bound).astype(kind)


def setup_inputs(seed: int = 0) -> dict:
    key_of = jax.random.split(jax.random.key(seed), 12)
    latents = gaussian(key_of[0], (STEPS, TOKENS, D), 1.0, 6.0, ((0, 8), (1, 16)))
    timesteps = set_ends(jax.random.randint(key_of[1], (SCHED,), 0, NT), jax.random.fold_in(key_of[1], 1), 0, NT - 1).astype(jnp.int32)
    experts = set_ends(jax.random.randint(key_of[2], (SCHED,), 0, 2), jax.random.fold_in(key_of[2], 1), 0, 1).astype(jnp.int32)
    offset = jax.random.randint(key_of[3], (1,), 0, SCHED - STEPS + 1).astype(jnp.int32)
    modulation = gaussian(key_of[4], (NT, 3, D), 1.0, 4.0, (), jnp.float32)
    coef = jnp.clip(jnp.exp(jax.random.uniform(key_of[5], (NT,), jnp.float32, math.log(0.1), math.log(1.0))), 0.1, 1.0)
    w_qkv = draw_w_qkv(jax.random.fold_in(key_of[11], 71), 0)
    w_o = gaussian(key_of[7], (2, D, D), D ** -0.5, 0.1875, ((1, 16),))
    w_cq = gaussian(key_of[8], (2, D, D), D ** -0.5, 0.1875, ((2, 16),))
    w_co = gaussian(key_of[9], (2, D, D), D ** -0.5, 0.1875, ((1, 16),))
    text_kv = draw_text_kv(jax.random.fold_in(key_of[11], 71), 0)
    return {"latents": latents, "timesteps": timesteps, "experts": experts, "offset": offset, "modulation": modulation, "coef": coef, "w_qkv": w_qkv, "w_o": w_o, "w_cq": w_cq, "w_co": w_co, "text_kv": text_kv}


def attend(queries, keys, values):
    scale = 1.0 / queries.shape[-1] ** 0.5
    scores = jnp.einsum('qhc,khc->hqk', queries.astype(jnp.float32), keys.astype(jnp.float32)) * scale
    scores = scores - lax.optimization_barrier(jnp.max(scores, axis=-1, keepdims=True))
    expsc = jnp.exp(scores)
    total = lax.optimization_barrier(jnp.sum(expsc, axis=-1))
    rounded = lax.optimization_barrier(expsc.astype(jnp.bfloat16)).astype(jnp.float32)
    out = jnp.einsum('hqk,khc->qhc', rounded, values.astype(jnp.float32))
    return (out / jnp.transpose(total)[:, :, None]).astype(jnp.bfloat16)

def blocked(queries, keys, values):
    count = queries.shape[0]
    block_rows = min(512, count)
    shaped = queries.reshape(count // block_rows, block_rows, queries.shape[1], queries.shape[2])
    result = lax.map(lambda part: attend(part, keys, values), shaped)
    return result.reshape(count, queries.shape[1], queries.shape[2])

def block_layer(latent, modulate, wqkv, wout, wcq, wco, textkv):
    width = latent.shape[1]
    heads = wqkv.shape[1]
    head_size = wqkv.shape[2] // 3
    flat = latent.astype(jnp.float32)
    mean = lax.optimization_barrier(jnp.mean(flat, axis=1, keepdims=True))
    var = lax.optimization_barrier(jnp.mean((flat - mean) ** 2, axis=1, keepdims=True))
    normed = ((flat - mean) * lax.rsqrt(var + 1e-06) * (1.0 + modulate[1]) + modulate[0]).astype(jnp.bfloat16)
    qkv = jnp.einsum('td,dhc->thc', normed.astype(jnp.float32), wqkv.astype(jnp.float32)).astype(jnp.bfloat16)
    attended = blocked(qkv[:, :, :head_size], qkv[:, :, head_size:2 * head_size], qkv[:, :, 2 * head_size:])
    attended = attended.reshape(-1, width)
    hidden = (flat + modulate[2] * jnp.dot(attended, wout, preferred_element_type=jnp.float32)).astype(jnp.bfloat16)
    cross_q = jnp.dot(hidden, wcq, preferred_element_type=jnp.float32).astype(jnp.bfloat16)
    text_keys = textkv[0].reshape(-1, heads, head_size)
    text_values = textkv[1].reshape(-1, heads, head_size)
    cross_out = blocked(cross_q.reshape(-1, heads, head_size), text_keys, text_values).reshape(-1, width)
    return (hidden.astype(jnp.float32) + jnp.dot(cross_out, wco, preferred_element_type=jnp.float32)).astype(jnp.bfloat16)

def reference(latents, timesteps, experts, offset, modulation, coef, w_qkv, w_o, w_cq, w_co, text_kv):
    running = latents[0].astype(jnp.float32)
    outputs = []
    for step in range(STEPS):
        position = offset[0] + step
        entry = timesteps[position]
        expert = experts[position]
        predicted = block_layer(latents[step], modulation[entry], w_qkv[expert], w_o[expert], w_cq[expert], w_co[expert], text_kv[expert])
        running = running + coef[entry] * predicted.astype(jnp.float32)
        outputs.append(running.astype(jnp.bfloat16))
    return jnp.stack(outputs, axis=0)
```

```python
import functools
import math

import jax
import jax.numpy as jnp
from jax import lax
from jax.experimental import pallas as pl
from jax.experimental.pallas import tpu as pltpu
from jax.sharding import PartitionSpec as P

HEAD = 72
LANES = 128
TEXT = 300
TEXT_PAD = 384
CHUNKS = (384, 128)
SOURCES = (2, 4)
ROW_BLOCK = 512
KEY_BLOCK = 1024
VALUE = 2 * HEAD - LANES
FACTOR = math.log2(math.e) / HEAD**0.5
VMEM_LIMIT = 60 * 2**20
def link_kernel(passed, *refs):
    del passed, refs


def link(values, after):
    values = list(values)
    return pl.pallas_call(
        functools.partial(link_kernel, len(values)),
        in_specs=[pl.BlockSpec(memory_space=pl.ANY)] * (len(values) + len(after)),
        out_specs=[pl.BlockSpec(memory_space=pl.ANY)] * len(values),
        out_shape=[jax.ShapeDtypeStruct(value.shape, value.dtype) for value in values],
        input_output_aliases={index: index for index in range(len(values))},
        compiler_params=pltpu.CompilerParams(vmem_limit_bytes=VMEM_LIMIT),
        name="link",
    )(*values, *after)


def whole(array):
    return pl.BlockSpec(array.shape, lambda *_: (0,) * len(array.shape))


def project_kernel(waited, *refs):
    rows, weights, queries, keys, values = refs[waited:]
    contract = (((1,), (1,)), ((), ()))
    mixed = lax.dot_general(
        rows[...], weights[...], contract, preferred_element_type=jnp.float32
    )
    low, high = mixed[:, :LANES], mixed[:, LANES:]
    queries[...] = low.astype(jnp.bfloat16)
    lane = lax.broadcasted_iota(jnp.int32, high.shape, 1)
    values[...] = jnp.where(lane >= VALUE + HEAD, 1.0, high).astype(jnp.bfloat16)
    pad = jnp.zeros((LANES - HEAD, mixed.shape[0]), jnp.float32)
    keys[...] = jnp.concatenate([low.T[HEAD:], high.T[:VALUE], pad], 0).astype(jnp.bfloat16)


def project(tokens, weights, after):
    count, width = tokens.shape
    flat = jax.ShapeDtypeStruct((count, LANES), jnp.bfloat16)
    turned = jax.ShapeDtypeStruct((LANES, count), jnp.bfloat16)
    flat_spec = pl.BlockSpec((ROW_BLOCK, LANES), lambda i: (i, 0))
    return pl.pallas_call(
        functools.partial(project_kernel, len(after)),
        grid=(count // ROW_BLOCK,),
        in_specs=[pl.BlockSpec(memory_space=pl.ANY)] * len(after)
        + [pl.BlockSpec((ROW_BLOCK, width), lambda i: (i, 0)), whole(weights)],
        out_specs=[flat_spec, pl.BlockSpec((LANES, ROW_BLOCK), lambda i: (0, i)), flat_spec],
        out_shape=(flat, turned, flat),
        compiler_params=pltpu.CompilerParams(vmem_limit_bytes=VMEM_LIMIT),
        cost_estimate=pl.CostEstimate(
            flops=4 * count * width * LANES,
            bytes_accessed=count * width * 2 + count * 6 * LANES,
            transcendentals=0,
        ),
        name="project",
    )(*after, tokens, weights)


def attend_kernel(waited, key_chunks, carried, final, *refs):
    refs = list(refs)[waited:]
    query_ref = refs.pop(0)
    keys = refs[:key_chunks]
    values = refs[key_chunks : 2 * key_chunks]
    del refs[: 2 * key_chunks]
    state = refs.pop(0) if carried else None
    out, scores = refs
    parts = [
        (key, value, slice(start, start + KEY_BLOCK))
        for key, value in zip(keys, values)
        for start in range(0, key.shape[1], KEY_BLOCK)
    ]
    query = query_ref[...]

    def score(step):
        key, _, span = parts[step]
        return jnp.dot(query, key[:, span], preferred_element_type=jnp.float32)

    if carried:
        total = state[...]
        top = total[:, LANES - 1 :]
    else:
        total = top = None
    scores[0] = score(0)
    for step in range(len(parts)):
        if step + 1 < len(parts):
            scores[(step + 1) % 2] = score(step + 1)
        now = scores[step % 2]
        high = jnp.max(now, axis=1, keepdims=True)
        newer = high if top is None else jnp.maximum(top, high)
        weights = jnp.exp2(now * FACTOR - newer * FACTOR).astype(jnp.bfloat16)
        _, value, span = parts[step]
        part = jnp.dot(weights, value[span, :], preferred_element_type=jnp.float32)
        total = part if top is None else total * jnp.exp2((top - newer) * FACTOR) + part
        top = newer
    if final:
        turned = total.T
        done = turned[VALUE : VALUE + HEAD] / turned[VALUE + HEAD : VALUE + HEAD + 1]
        per = out.shape[2]
        for piece in range(out.shape[0]):
            out[piece] = done[:, piece * per : (piece + 1) * per].astype(jnp.bfloat16)
    else:
        lane = lax.broadcasted_iota(jnp.int32, total.shape, 1)
        out[...] = jnp.where(lane == LANES - 1, top, total)


def attend_chunk(queries, per, together, sources, state, final, after):
    count = queries.shape[0]
    block = per * together
    row_spec = pl.BlockSpec((block, LANES), lambda i: (i, 0))
    args = [*after, queries]
    in_specs = [pl.BlockSpec(memory_space=pl.ANY)] * len(after) + [row_spec]
    for index in (1, 2):
        args += [chunk[index] for chunk in sources]
        in_specs += [whole(chunk[index]) for chunk in sources]
    if state is not None:
        args.append(state)
        in_specs.append(row_spec)
    if final:
        out_shape = jax.ShapeDtypeStruct((count // per, HEAD, per), jnp.bfloat16)
        out_spec = pl.BlockSpec((together, HEAD, per), lambda i: (i, 0, 0))
    else:
        out_shape = jax.ShapeDtypeStruct((count, LANES), jnp.float32)
        out_spec = row_spec
    pairs = count * sum(chunk[1].shape[1] for chunk in sources)
    return pl.pallas_call(
        functools.partial(attend_kernel, len(after), len(sources), state is not None, final),
        grid=(count // block,),
        in_specs=in_specs,
        out_specs=out_spec,
        scratch_shapes=[pltpu.VMEM((2, block, KEY_BLOCK), jnp.float32)],
        out_shape=out_shape,
        compiler_params=pltpu.CompilerParams(vmem_limit_bytes=VMEM_LIMIT),
        cost_estimate=pl.CostEstimate(
            flops=4 * pairs * LANES * 2, bytes_accessed=4 * 2**20, transcendentals=pairs
        ),
        name="self_attend",
    )(*args)


def self_attend(normed, weights, early):
    chunks, states, previous, start = [], [], [], 0
    held = None
    for chunk, per in enumerate(CHUNKS):
        own = normed[start : start + per]
        start += per
        if held is not None:
            own = link([own], [held])[0]
        held = lax.all_gather(own, "tok", axis=0, tiled=True)
        chunks.append([held])
    for chunk, per in enumerate(CHUNKS):
        last = chunk + 1 == len(CHUNKS)
        chunks[chunk] = project(chunks[chunk][0], weights, previous + early[chunk])
        for earlier in range(chunk + 1):
            before = states[earlier] if earlier < chunk else None
            keys = chunks[chunk : chunk + 1] if earlier < chunk else chunks[: chunk + 1]
            result = attend_chunk(
                chunks[earlier][0], CHUNKS[earlier], SOURCES[earlier], keys, before, last, previous
            )
            previous = [result]
            states[earlier : earlier + 1] = [result]
    return states, chunks


def finish_kernel(parts, *refs):
    turned, (latent, gate, weights, keys, values, out, cross) = refs[:parts], refs[parts:]
    width = latent.shape[1]

    def weight(index):
        return weights[:, index].astype(jnp.float32).reshape(width, width).astype(jnp.bfloat16)

    attended = jnp.concatenate([part[...].astype(jnp.float32) for part in turned], 1)
    attended = attended.T.astype(jnp.bfloat16)
    projected = jnp.dot(attended, weight(0), preferred_element_type=jnp.float32)
    hidden = (latent[...].astype(jnp.float32) + gate[...] * projected).astype(jnp.bfloat16)
    queries = lax.dot_general(
        weight(1), hidden, (((1,), (1,)), ((), ())), preferred_element_type=jnp.float32
    )
    for head in range(width // HEAD):
        rows = slice(head * HEAD, (head + 1) * HEAD)
        scores = jnp.dot(
            keys[head], queries[rows].astype(jnp.bfloat16), preferred_element_type=jnp.float32
        )
        row = lax.broadcasted_iota(jnp.int32, scores.shape, 0)
        scores = jnp.where(row < TEXT, scores, -jnp.inf)
        high = jnp.max(scores, axis=0, keepdims=True)
        exps = jnp.exp2((scores - high) * FACTOR)
        total = jnp.sum(exps, axis=0, keepdims=True)
        result = jnp.dot(
            values[head], exps.astype(jnp.bfloat16), preferred_element_type=jnp.float32
        )
        cross[rows, :] = result / total
    crossed = cross[...].T.astype(jnp.bfloat16)
    out[...] = (
        hidden.astype(jnp.float32)
        + jnp.dot(crossed, weight(2), preferred_element_type=jnp.float32)
    ).astype(jnp.bfloat16)


def finish(turned, latent, gate, weights, keys, values):
    count, width = latent.shape
    args = (*turned, latent, gate, weights, keys, values)
    return pl.pallas_call(
        functools.partial(finish_kernel, len(turned)),
        grid=(1,),
        in_specs=[whole(arg) for arg in args],
        out_specs=whole(latent),
        out_shape=jax.ShapeDtypeStruct((count, width), jnp.bfloat16),
        scratch_shapes=[pltpu.VMEM((width, count), jnp.float32)],
        compiler_params=pltpu.CompilerParams(vmem_limit_bytes=VMEM_LIMIT),
        cost_estimate=pl.CostEstimate(
            flops=10 * count * width * width, bytes_accessed=10 * 2**20, transcendentals=0
        ),
        name="finish",
    )(*args)


def scan_kernel(coefs, first, everyone, out):
    running = first[...].astype(jnp.float32)
    for step in range(everyone.shape[0]):
        running = running + coefs[step] * everyone[step].astype(jnp.float32)
        out[step] = running.astype(jnp.bfloat16)


def scan(coefs, first, everyone):
    return pl.pallas_call(
        scan_kernel,
        grid_spec=pltpu.PrefetchScalarGridSpec(
            num_scalar_prefetch=1,
            grid=(1,),
            in_specs=[whole(first), whole(everyone)],
            out_specs=whole(everyone),
        ),
        out_shape=jax.ShapeDtypeStruct(everyone.shape, jnp.bfloat16),
        compiler_params=pltpu.CompilerParams(vmem_limit_bytes=VMEM_LIMIT),
        name="scan",
    )(coefs, first, everyone)


def body(latents, timesteps, experts, offset, modulation, coef, w_qkv, w_o, w_cq, w_co, text_kv):
    step_index = lax.axis_index("step")
    steps = lax.axis_size("step")
    position = offset[0] + step_index
    entry = lax.dynamic_index_in_dim(timesteps, position, 0, False)
    expert = lax.dynamic_index_in_dim(experts, position, 0, False)
    modulate = lax.dynamic_index_in_dim(modulation, entry, 0, False)
    latent = latents[0]
    count, width = latent.shape
    heads = width // HEAD
    flat = latent.astype(jnp.float32)
    mean = jnp.mean(flat, axis=1, keepdims=True)
    var = jnp.mean((flat - mean) ** 2, axis=1, keepdims=True)
    normed = ((flat - mean) * lax.rsqrt(var + 1e-06) * (1.0 + modulate[1]) + modulate[0]).astype(
        jnp.bfloat16
    )
    own_qkv = jnp.swapaxes(lax.dynamic_index_in_dim(w_qkv, expert, 0, False)[:, 0, :], 0, 1)
    w_mixed = jnp.pad(own_qkv, ((0, 2 * LANES - 3 * HEAD), (0, 0)))

    def over_steps(value):
        shaped = value.reshape(steps, -1, width)
        return lax.all_to_all(shaped, "step", split_axis=0, concat_axis=0, tiled=True)

    first = over_steps(latent)[0]
    own_text = lax.dynamic_index_in_dim(text_kv, expert, 0, False).reshape(2, TEXT, heads, HEAD)
    text_keys = jnp.pad(
        jnp.transpose(own_text[0], (1, 0, 2)), ((0, 0), (0, TEXT_PAD - TEXT), (0, 0))
    )
    text_values = jnp.pad(
        jnp.transpose(own_text[1], (1, 2, 0)), ((0, 0), (0, 0), (0, TEXT_PAD - TEXT))
    )
    first, text_keys, text_values = link([first, text_keys, text_values], [])
    own_weights = jnp.stack(
        [
            lax.dynamic_index_in_dim(w_o, expert, 0, False),
            jnp.swapaxes(lax.dynamic_index_in_dim(w_cq, expert, 0, False), 0, 1),
            lax.dynamic_index_in_dim(w_co, expert, 0, False),
        ]
    )
    heads_out, chunks = self_attend(
        normed, w_mixed, ([first], [text_keys, text_values, own_weights])
    )
    all_weights = lax.all_gather(
        link([own_weights], [chunks[0][0]])[0], "tok", axis=0, tiled=False
    )

    def returned(value):
        back = lax.all_to_all(value, "tok", split_axis=0, concat_axis=0, tiled=True)
        return back.reshape(width, -1)

    turned = [returned(heads_out[0])]
    turned.append(returned(link([heads_out[1]], turned)[0]))
    predicted = finish(turned, latent, modulate[2][None], all_weights, text_keys, text_values)
    coefs = jnp.take(coef, lax.dynamic_slice_in_dim(timesteps, offset[0], steps))
    return over_steps(scan(coefs, first, over_steps(predicted))).reshape(1, count, width)


def solution(mesh):
    in_specs = (
        P("step", "tok", None),
        P(),
        P(),
        P(),
        P(),
        P(),
        P(None, None, "tok", None),
        P(None, "tok", None),
        P(None, None, "tok"),
        P(None, "tok", None),
        P(),
    )
    out_specs = P("step", "tok", None)
    return jax.shard_map(body, mesh=mesh, in_specs=in_specs, out_specs=out_specs, check_vma=False)
```

```python
import functools
import math

import jax
import jax.numpy as jnp
from jax import lax
from jax.experimental import pallas as pl
from jax.experimental.pallas import tpu as pltpu
from jax.sharding import PartitionSpec as P

HEAD = 72
LANES = 128
TEXT = 300
TEXT_PAD = 384
CHUNKS = (384, 128)
SOURCES = (2, 8)
ROW_BLOCK = 1024
KEY_BLOCK = 1024
HALVES = 2
VALUE = 2 * HEAD - LANES
FACTOR = math.log2(math.e) / HEAD**0.5
VMEM_LIMIT = 60 * 2**20
def link_kernel(passed, *refs):
    del passed, refs


def link(values, after):
    values = list(values)
    return pl.pallas_call(
        functools.partial(link_kernel, len(values)),
        in_specs=[pl.BlockSpec(memory_space=pl.ANY)] * (len(values) + len(after)),
        out_specs=[pl.BlockSpec(memory_space=pl.ANY)] * len(values),
        out_shape=[jax.ShapeDtypeStruct(value.shape, value.dtype) for value in values],
        input_output_aliases={index: index for index in range(len(values))},
        compiler_params=pltpu.CompilerParams(vmem_limit_bytes=VMEM_LIMIT),
        name="link",
    )(*values, *after)


def whole(array):
    return pl.BlockSpec(array.shape, lambda *_: (0,) * len(array.shape))


def project_kernel(waited, *refs):
    rows, weights, queries, keys, values = refs[waited:]
    mixed = jnp.dot(rows[...], weights[...], preferred_element_type=jnp.float32)
    low, high = mixed[:, :LANES], mixed[:, LANES:]
    queries[...] = low.astype(jnp.bfloat16)
    lane = lax.broadcasted_iota(jnp.int32, high.shape, 1)
    values[...] = jnp.where(lane >= VALUE + HEAD, 1.0, high).astype(jnp.bfloat16)
    pad = jnp.zeros((LANES - HEAD, mixed.shape[0]), jnp.float32)
    keys[...] = jnp.concatenate([low.T[HEAD:], high.T[:VALUE], pad], 0).astype(jnp.bfloat16)


def project(tokens, weights, after):
    count, width = tokens.shape
    flat = jax.ShapeDtypeStruct((count, LANES), jnp.bfloat16)
    turned = jax.ShapeDtypeStruct((LANES, count), jnp.bfloat16)
    flat_spec = pl.BlockSpec((ROW_BLOCK, LANES), lambda i: (i, 0))
    return pl.pallas_call(
        functools.partial(project_kernel, len(after)),
        grid=(count // ROW_BLOCK,),
        in_specs=[pl.BlockSpec(memory_space=pl.ANY)] * len(after)
        + [pl.BlockSpec((ROW_BLOCK, width), lambda i: (i, 0)), whole(weights)],
        out_specs=[flat_spec, pl.BlockSpec((LANES, ROW_BLOCK), lambda i: (0, i)), flat_spec],
        out_shape=(flat, turned, flat),
        compiler_params=pltpu.CompilerParams(vmem_limit_bytes=VMEM_LIMIT),
        cost_estimate=pl.CostEstimate(
            flops=4 * count * width * LANES,
            bytes_accessed=count * width * 2 + count * 6 * LANES,
            transcendentals=0,
        ),
        name="project",
    )(*after, tokens, weights)


def attend_kernel(waited, key_chunks, carried, final, *refs):
    refs = list(refs)[waited:]
    query_ref = refs.pop(0)
    keys = refs[:key_chunks]
    values = refs[key_chunks : 2 * key_chunks]
    del refs[: 2 * key_chunks]
    state = refs.pop(0) if carried else None
    out, scores = refs
    parts = [
        (key, value, slice(start, start + KEY_BLOCK))
        for key, value in zip(keys, values)
        for start in range(0, key.shape[1], KEY_BLOCK)
    ]
    rows = query_ref.shape[0] // HALVES
    spans = [slice(half * rows, (half + 1) * rows) for half in range(HALVES)]
    units = [(half, step) for step in range(len(parts)) for half in range(HALVES)]

    def score(unit):
        half, step = unit
        key, _, span = parts[step]
        return jnp.dot(
            query_ref[spans[half], :], key[:, span], preferred_element_type=jnp.float32
        )

    totals = [state[span, :] if carried else None for span in spans]
    tops = [total[:, LANES - 1 :] if carried else None for total in totals]
    scores[0] = score(units[0])
    for index, (half, step) in enumerate(units):
        if index + 1 < len(units):
            scores[(index + 1) % 2] = score(units[index + 1])
        now = scores[index % 2]
        top, total = tops[half], totals[half]
        high = jnp.max(now, axis=1, keepdims=True)
        newer = high if top is None else jnp.maximum(top, high)
        weights = jnp.exp2(now * FACTOR - newer * FACTOR).astype(jnp.bfloat16)
        _, value, span = parts[step]
        part = jnp.dot(weights, value[span, :], preferred_element_type=jnp.float32)
        totals[half] = part if top is None else total * jnp.exp2((top - newer) * FACTOR) + part
        tops[half] = newer
    for half, (total, top) in enumerate(zip(totals, tops)):
        if final:
            turned = total.T
            done = turned[VALUE : VALUE + HEAD] / turned[VALUE + HEAD : VALUE + HEAD + 1]
            per = out.shape[2]
            for piece in range(rows // per):
                out[half * (rows // per) + piece] = done[
                    :, piece * per : (piece + 1) * per
                ].astype(jnp.bfloat16)
        else:
            lane = lax.broadcasted_iota(jnp.int32, total.shape, 1)
            out[spans[half], :] = jnp.where(lane == LANES - 1, top, total)


def attend_chunk(queries, per, together, sources, state, final, after):
    count = queries.shape[0]
    block = per * together
    row_spec = pl.BlockSpec((block, LANES), lambda i: (i, 0))
    args = [*after, queries]
    in_specs = [pl.BlockSpec(memory_space=pl.ANY)] * len(after) + [row_spec]
    for index in (1, 2):
        args += [chunk[index] for chunk in sources]
        in_specs += [whole(chunk[index]) for chunk in sources]
    if state is not None:
        args.append(state)
        in_specs.append(row_spec)
    if final:
        out_shape = jax.ShapeDtypeStruct((count // per, HEAD, per), jnp.bfloat16)
        out_spec = pl.BlockSpec((together, HEAD, per), lambda i: (i, 0, 0))
    else:
        out_shape = jax.ShapeDtypeStruct((count, LANES), jnp.float32)
        out_spec = row_spec
    pairs = count * sum(chunk[1].shape[1] for chunk in sources)
    return pl.pallas_call(
        functools.partial(attend_kernel, len(after), len(sources), state is not None, final),
        grid=(count // block,),
        in_specs=in_specs,
        out_specs=out_spec,
        scratch_shapes=[pltpu.VMEM((2, block // HALVES, KEY_BLOCK), jnp.float32)],
        out_shape=out_shape,
        compiler_params=pltpu.CompilerParams(vmem_limit_bytes=VMEM_LIMIT),
        cost_estimate=pl.CostEstimate(
            flops=4 * pairs * LANES * 2, bytes_accessed=4 * 2**20, transcendentals=pairs
        ),
        name="self_attend",
    )(*args)


def self_attend(normed, weights, early):
    chunks, states, previous, start = [], [], [], 0
    held = None
    for chunk, per in enumerate(CHUNKS):
        own = normed[start : start + per]
        start += per
        if held is not None:
            own = link([own], [held] + early[chunk])[0]
        held = lax.all_gather(own, "tok", axis=0, tiled=True)
        chunks.append([held])
    for chunk, per in enumerate(CHUNKS):
        last = chunk + 1 == len(CHUNKS)
        chunks[chunk] = project(chunks[chunk][0], weights, previous)
        for earlier in range(chunk + 1):
            before = states[earlier] if earlier < chunk else None
            keys = chunks[chunk : chunk + 1] if earlier < chunk else chunks[: chunk + 1]
            result = attend_chunk(
                chunks[earlier][0], CHUNKS[earlier], SOURCES[earlier], keys, before, last, previous
            )
            previous = [result]
            states[earlier : earlier + 1] = [result]
    return states, chunks


def finish_kernel(parts, *refs):
    turned, (latent, gate, weights, keys, values, out, cross) = refs[:parts], refs[parts:]
    width = latent.shape[1]

    def weight(index):
        return weights[:, index].astype(jnp.float32).reshape(width, width).astype(jnp.bfloat16)

    attended = jnp.concatenate([part[...].astype(jnp.float32) for part in turned], 1)
    attended = attended.T.astype(jnp.bfloat16)
    projected = jnp.dot(attended, weight(0), preferred_element_type=jnp.float32)
    hidden = (latent[...].astype(jnp.float32) + gate[...] * projected).astype(jnp.bfloat16)
    queries = lax.dot_general(
        weight(1), hidden, (((1,), (1,)), ((), ())), preferred_element_type=jnp.float32
    )
    for head in range(width // HEAD):
        rows = slice(head * HEAD, (head + 1) * HEAD)
        scores = jnp.dot(
            keys[head], queries[rows].astype(jnp.bfloat16), preferred_element_type=jnp.float32
        )
        row = lax.broadcasted_iota(jnp.int32, scores.shape, 0)
        scores = jnp.where(row < TEXT, scores, -jnp.inf)
        high = jnp.max(scores, axis=0, keepdims=True)
        exps = jnp.exp2((scores - high) * FACTOR)
        total = jnp.sum(exps, axis=0, keepdims=True)
        result = jnp.dot(
            values[head], exps.astype(jnp.bfloat16), preferred_element_type=jnp.float32
        )
        cross[rows, :] = result / total
    crossed = cross[...].T.astype(jnp.bfloat16)
    out[...] = (
        hidden.astype(jnp.float32)
        + jnp.dot(crossed, weight(2), preferred_element_type=jnp.float32)
    ).astype(jnp.bfloat16)


def finish(turned, latent, gate, weights, keys, values):
    count, width = latent.shape
    args = (*turned, latent, gate, weights, keys, values)
    return pl.pallas_call(
        functools.partial(finish_kernel, len(turned)),
        grid=(1,),
        in_specs=[whole(arg) for arg in args],
        out_specs=whole(latent),
        out_shape=jax.ShapeDtypeStruct((count, width), jnp.bfloat16),
        scratch_shapes=[pltpu.VMEM((width, count), jnp.float32)],
        compiler_params=pltpu.CompilerParams(vmem_limit_bytes=VMEM_LIMIT),
        cost_estimate=pl.CostEstimate(
            flops=10 * count * width * width, bytes_accessed=10 * 2**20, transcendentals=0
        ),
        name="finish",
    )(*args)


def scan_kernel(coefs, first, everyone, out):
    running = first[...].astype(jnp.float32)
    for step in range(everyone.shape[0]):
        running = running + coefs[step] * everyone[step].astype(jnp.float32)
        out[step] = running.astype(jnp.bfloat16)


def scan(coefs, first, everyone):
    return pl.pallas_call(
        scan_kernel,
        grid_spec=pltpu.PrefetchScalarGridSpec(
            num_scalar_prefetch=1,
            grid=(1,),
            in_specs=[whole(first), whole(everyone)],
            out_specs=whole(everyone),
        ),
        out_shape=jax.ShapeDtypeStruct(everyone.shape, jnp.bfloat16),
        compiler_params=pltpu.CompilerParams(vmem_limit_bytes=VMEM_LIMIT),
        name="scan",
    )(coefs, first, everyone)


def body(latents, timesteps, experts, offset, modulation, coef, w_qkv, w_o, w_cq, w_co, text_kv):
    step_index = lax.axis_index("step")
    steps = lax.axis_size("step")
    position = offset[0] + step_index
    entry = lax.dynamic_index_in_dim(timesteps, position, 0, False)
    expert = lax.dynamic_index_in_dim(experts, position, 0, False)
    modulate = lax.dynamic_index_in_dim(modulation, entry, 0, False)
    latent = latents[0]
    count, width = latent.shape
    heads = width // HEAD
    flat = latent.astype(jnp.float32)
    mean = jnp.mean(flat, axis=1, keepdims=True)
    var = jnp.mean((flat - mean) ** 2, axis=1, keepdims=True)
    normed = ((flat - mean) * lax.rsqrt(var + 1e-06) * (1.0 + modulate[1]) + modulate[0]).astype(
        jnp.bfloat16
    )
    own_qkv = lax.dynamic_index_in_dim(w_qkv, expert, 0, False)[:, 0, :]
    w_mixed = jnp.pad(own_qkv, ((0, 0), (0, 2 * LANES - 3 * HEAD)))

    def over_steps(value):
        shaped = value.reshape(steps, -1, width)
        return lax.all_to_all(shaped, "step", split_axis=0, concat_axis=0, tiled=True)

    first = over_steps(latent)[0]
    own_text = lax.dynamic_index_in_dim(text_kv, expert, 0, False).reshape(2, TEXT, heads, HEAD)
    text_keys = jnp.pad(
        jnp.transpose(own_text[0], (1, 0, 2)), ((0, 0), (0, TEXT_PAD - TEXT), (0, 0))
    )
    text_values = jnp.pad(
        jnp.transpose(own_text[1], (1, 2, 0)), ((0, 0), (0, 0), (0, TEXT_PAD - TEXT))
    )
    first, text_keys, text_values = link([first, text_keys, text_values], [])
    own_weights = jnp.stack(
        [
            lax.dynamic_index_in_dim(w_o, expert, 0, False),
            jnp.swapaxes(lax.dynamic_index_in_dim(w_cq, expert, 0, False), 0, 1),
            lax.dynamic_index_in_dim(w_co, expert, 0, False),
        ]
    )
    heads_out, chunks = self_attend(
        normed, w_mixed, ([], [first, text_keys, text_values, own_weights, w_mixed])
    )
    all_weights = lax.all_gather(
        link([own_weights], [chunks[0][0]])[0], "tok", axis=0, tiled=False
    )

    def returned(value):
        back = lax.all_to_all(value, "tok", split_axis=0, concat_axis=0, tiled=True)
        return back.reshape(width, -1)

    turned = [returned(heads_out[0])]
    turned.append(returned(link([heads_out[1]], turned)[0]))
    predicted = finish(turned, latent, modulate[2][None], all_weights, text_keys, text_values)
    coefs = jnp.take(coef, lax.dynamic_slice_in_dim(timesteps, offset[0], steps))
    return over_steps(scan(coefs, first, over_steps(predicted))).reshape(1, count, width)


def solution(mesh):
    in_specs = (
        P("step", "tok", None),
        P(),
        P(),
        P(),
        P(),
        P(),
        P(None, None, "tok", None),
        P(None, "tok", None),
        P(None, None, "tok"),
        P(None, "tok", None),
        P(),
    )
    out_specs = P("step", "tok", None)
    return jax.shard_map(body, mesh=mesh, in_specs=in_specs, out_specs=out_specs, check_vma=False)
```

```python
import functools
import math

import jax
import jax.numpy as jnp
from jax import lax
from jax.experimental import pallas as pl
from jax.experimental.pallas import tpu as pltpu
from jax.sharding import PartitionSpec as P

HEAD = 72
LANES = 128
TEXT = 300
TEXT_PAD = 384
CHUNKS = (384, 128)
SOURCES = (2, 8)
ROW_BLOCK = 1024
ROWS = 128
KEY_BLOCK = 1024
HALVES = 2
STRIP = 32
VALUE = 2 * HEAD - LANES
FACTOR = math.log2(math.e) / HEAD**0.5
VMEM_LIMIT = 60 * 2**20
def link_kernel(passed, *refs):
    del passed, refs


def link(values, after):
    values = list(values)
    return pl.pallas_call(
        functools.partial(link_kernel, len(values)),
        in_specs=[pl.BlockSpec(memory_space=pl.ANY)] * (len(values) + len(after)),
        out_specs=[pl.BlockSpec(memory_space=pl.ANY)] * len(values),
        out_shape=[jax.ShapeDtypeStruct(value.shape, value.dtype) for value in values],
        input_output_aliases={index: index for index in range(len(values))},
        compiler_params=pltpu.CompilerParams(vmem_limit_bytes=VMEM_LIMIT),
        name="link",
    )(*values, *after)


def whole(array):
    return pl.BlockSpec(array.shape, lambda *_: (0,) * len(array.shape))


def norm_kernel(entry, latent, modulation, *outs):
    flat = latent[...].astype(jnp.float32)
    mean = jnp.mean(flat, axis=1, keepdims=True)
    centred = flat - mean
    var = jnp.mean(centred**2, axis=1, keepdims=True)
    row = pl.ds(entry[0] % 8, 1)
    shift, scale = modulation[0, row, :], modulation[1, row, :]
    normed = (centred * lax.rsqrt(var + 1e-06) * (1.0 + scale) + shift).astype(jnp.bfloat16)
    here = pl.program_id(0)
    first = CHUNKS[0] // ROWS

    @pl.when(here < first)
    def _():
        outs[0][...] = normed

    @pl.when(here >= first)
    def _():
        outs[1][...] = normed


def norm(latent, modulation, entry):
    count, width = latent.shape
    first = CHUNKS[0] // ROWS
    block = (ROWS, width)
    return pl.pallas_call(
        norm_kernel,
        grid_spec=pltpu.PrefetchScalarGridSpec(
            num_scalar_prefetch=1,
            grid=(count // ROWS,),
            in_specs=[
                pl.BlockSpec(block, lambda i, entry: (i, 0)),
                pl.BlockSpec((3, 8, width), lambda i, entry: (0, entry[0] // 8, 0)),
            ],
            out_specs=[
                pl.BlockSpec(block, lambda i, entry: (jnp.minimum(i, first - 1), 0)),
                pl.BlockSpec(block, lambda i, entry: (jnp.maximum(i - first, 0), 0)),
            ],
        ),
        out_shape=[jax.ShapeDtypeStruct((per, width), jnp.bfloat16) for per in CHUNKS],
        compiler_params=pltpu.CompilerParams(vmem_limit_bytes=VMEM_LIMIT),
        name="norm",
    )(entry, latent, modulation)


def project_kernel(waited, *refs):
    rows, weights, queries, keys, values = refs[waited:]
    mixed = jnp.dot(rows[...], weights[...], preferred_element_type=jnp.float32)
    low, high = mixed[:, :LANES], mixed[:, LANES:]
    queries[...] = low.astype(jnp.bfloat16)
    lane = lax.broadcasted_iota(jnp.int32, high.shape, 1)
    values[...] = jnp.where(lane >= VALUE + HEAD, 1.0, high).astype(jnp.bfloat16)
    pad = jnp.zeros((LANES - HEAD, mixed.shape[0]), jnp.float32)
    keys[...] = jnp.concatenate([low.T[HEAD:], high.T[:VALUE], pad], 0).astype(jnp.bfloat16)


def project(tokens, weights, after):
    count, width = tokens.shape
    flat = jax.ShapeDtypeStruct((count, LANES), jnp.bfloat16)
    turned = jax.ShapeDtypeStruct((LANES, count), jnp.bfloat16)
    flat_spec = pl.BlockSpec((ROW_BLOCK, LANES), lambda i: (i, 0))
    return pl.pallas_call(
        functools.partial(project_kernel, len(after)),
        grid=(count // ROW_BLOCK,),
        in_specs=[pl.BlockSpec(memory_space=pl.ANY)] * len(after)
        + [pl.BlockSpec((ROW_BLOCK, width), lambda i: (i, 0)), whole(weights)],
        out_specs=[flat_spec, pl.BlockSpec((LANES, ROW_BLOCK), lambda i: (0, i)), flat_spec],
        out_shape=(flat, turned, flat),
        compiler_params=pltpu.CompilerParams(vmem_limit_bytes=VMEM_LIMIT),
        cost_estimate=pl.CostEstimate(
            flops=4 * count * width * LANES,
            bytes_accessed=count * width * 2 + count * 6 * LANES,
            transcendentals=0,
        ),
        name="project",
    )(*after, tokens, weights)


def attend_kernel(waited, key_chunks, carried, final, *refs):
    refs = list(refs)[waited:]
    query_ref = refs.pop(0)
    keys = refs[:key_chunks]
    values = refs[key_chunks : 2 * key_chunks]
    del refs[: 2 * key_chunks]
    state = refs.pop(0) if carried else None
    out, scores, exps = refs
    parts = [
        (key, value, slice(start, start + KEY_BLOCK))
        for key, value in zip(keys, values)
        for start in range(0, key.shape[1], KEY_BLOCK)
    ]
    rows = query_ref.shape[0] // HALVES
    spans = [slice(half * rows, (half + 1) * rows) for half in range(HALVES)]
    units = [(half, step) for step in range(len(parts)) for half in range(HALVES)]

    def score(unit):
        half, step = unit
        key, _, span = parts[step]
        return jnp.dot(
            query_ref[spans[half], :], key[:, span], preferred_element_type=jnp.float32
        )

    strips = [slice(start, start + STRIP) for start in range(0, rows, STRIP)]
    totals = [state[span, :] if carried else None for span in spans]
    tops = [
        [total[strip, LANES - 1 :] if carried else None for strip in strips] for total in totals
    ]
    scores[0] = score(units[0])
    for index, (half, step) in enumerate(units):
        if index + 1 < len(units):
            scores[(index + 1) % 2] = score(units[index + 1])
        fresh = tops[half][0] is None
        shrink = []
        for place, strip in enumerate(strips):
            now = scores[index % 2, strip, :]
            top = tops[half][place]
            high = jnp.max(now, axis=1, keepdims=True)
            newer = high if fresh else jnp.maximum(top, high)
            exps[strip, :] = jnp.exp2(now * FACTOR - newer * FACTOR).astype(jnp.bfloat16)
            if not fresh:
                shrink.append(jnp.exp2((top - newer) * FACTOR))
            tops[half][place] = newer
        _, value, span = parts[step]
        part = jnp.dot(exps[...], value[span, :], preferred_element_type=jnp.float32)
        totals[half] = part if fresh else totals[half] * jnp.concatenate(shrink, 0) + part
    tops = [jnp.concatenate(top, 0) for top in tops]
    for half, (total, top) in enumerate(zip(totals, tops)):
        if final:
            turned = total.T
            done = turned[VALUE : VALUE + HEAD] / turned[VALUE + HEAD : VALUE + HEAD + 1]
            per = out.shape[2]
            for piece in range(rows // per):
                out[half * (rows // per) + piece] = done[
                    :, piece * per : (piece + 1) * per
                ].astype(jnp.bfloat16)
        else:
            lane = lax.broadcasted_iota(jnp.int32, total.shape, 1)
            out[spans[half], :] = jnp.where(lane == LANES - 1, top, total)


def attend_chunk(queries, per, together, sources, state, final, after):
    count = queries.shape[0]
    block = per * together
    row_spec = pl.BlockSpec((block, LANES), lambda i: (i, 0))
    args = [*after, queries]
    in_specs = [pl.BlockSpec(memory_space=pl.ANY)] * len(after) + [row_spec]
    for index in (1, 2):
        args += [chunk[index] for chunk in sources]
        in_specs += [whole(chunk[index]) for chunk in sources]
    if state is not None:
        args.append(state)
        in_specs.append(row_spec)
    if final:
        out_shape = jax.ShapeDtypeStruct((count // per, HEAD, per), jnp.bfloat16)
        out_spec = pl.BlockSpec((together, HEAD, per), lambda i: (i, 0, 0))
    else:
        out_shape = jax.ShapeDtypeStruct((count, LANES), jnp.float32)
        out_spec = row_spec
    pairs = count * sum(chunk[1].shape[1] for chunk in sources)
    return pl.pallas_call(
        functools.partial(attend_kernel, len(after), len(sources), state is not None, final),
        grid=(count // block,),
        in_specs=in_specs,
        out_specs=out_spec,
        scratch_shapes=[
            pltpu.VMEM((2, block // HALVES, KEY_BLOCK), jnp.float32),
            pltpu.VMEM((block // HALVES, KEY_BLOCK), jnp.bfloat16),
        ],
        out_shape=out_shape,
        compiler_params=pltpu.CompilerParams(vmem_limit_bytes=VMEM_LIMIT),
        cost_estimate=pl.CostEstimate(
            flops=4 * pairs * LANES * 2, bytes_accessed=4 * 2**20, transcendentals=pairs
        ),
        name="self_attend",
    )(*args)


def self_attend(normed, weights, early):
    chunks, states, previous = [], [], []
    held = None
    for chunk in range(len(CHUNKS)):
        own = normed[chunk]
        if held is not None:
            own = link([own], [held] + early[chunk])[0]
        held = lax.all_gather(own, "tok", axis=0, tiled=True)
        chunks.append([held])
    for chunk in range(len(CHUNKS)):
        last = chunk + 1 == len(CHUNKS)
        chunks[chunk] = project(chunks[chunk][0], weights, previous)
        for earlier in range(chunk + 1):
            before = states[earlier] if earlier < chunk else None
            keys = chunks[chunk : chunk + 1] if earlier < chunk else chunks[: chunk + 1]
            result = attend_chunk(
                chunks[earlier][0], CHUNKS[earlier], SOURCES[earlier], keys, before, last, previous
            )
            previous = [result]
            states[earlier : earlier + 1] = [result]
    return states, chunks


def finish_kernel(parts, *refs):
    turned, (latent, gate, weights, keys, values) = refs[:parts], refs[parts : parts + 5]
    out, cross, near, arrived = refs[parts + 5 :]
    width = latent.shape[1]
    copies = [
        pltpu.make_async_copy(weights.at[:, index], near.at[index], arrived.at[index])
        for index in range(3)
    ]
    for copy in copies:
        copy.start()

    def weight(index):
        copies[index].wait()
        return near[index].astype(jnp.float32).reshape(width, width).astype(jnp.bfloat16)

    attended = jnp.concatenate([part[...].astype(jnp.float32) for part in turned], 1)
    attended = attended.T.astype(jnp.bfloat16)
    projected = jnp.dot(attended, weight(0), preferred_element_type=jnp.float32)
    hidden = (latent[...].astype(jnp.float32) + gate[...] * projected).astype(jnp.bfloat16)
    queries = lax.dot_general(
        weight(1), hidden, (((1,), (1,)), ((), ())), preferred_element_type=jnp.float32
    )
    for head in range(width // HEAD):
        rows = slice(head * HEAD, (head + 1) * HEAD)
        scores = jnp.dot(
            keys[head], queries[rows].astype(jnp.bfloat16), preferred_element_type=jnp.float32
        )
        row = lax.broadcasted_iota(jnp.int32, scores.shape, 0)
        scores = jnp.where(row < TEXT, scores, -jnp.inf)
        high = jnp.max(scores, axis=0, keepdims=True)
        exps = jnp.exp2((scores - high) * FACTOR)
        total = jnp.sum(exps, axis=0, keepdims=True)
        result = jnp.dot(
            values[head], exps.astype(jnp.bfloat16), preferred_element_type=jnp.float32
        )
        cross[rows, :] = result / total
    crossed = cross[...].T.astype(jnp.bfloat16)
    out[...] = (
        hidden.astype(jnp.float32)
        + jnp.dot(crossed, weight(2), preferred_element_type=jnp.float32)
    ).astype(jnp.bfloat16)


def finish(turned, latent, gate, weights, keys, values):
    count, width = latent.shape
    heads = width // HEAD
    args = (*turned, latent, gate, weights, keys, values)
    return pl.pallas_call(
        functools.partial(finish_kernel, len(turned)),
        grid=(1,),
        in_specs=[
            pl.BlockSpec(memory_space=pl.ANY) if arg is weights else whole(arg) for arg in args
        ],
        out_specs=whole(latent),
        out_shape=jax.ShapeDtypeStruct((count, width), jnp.bfloat16),
        scratch_shapes=[
            pltpu.VMEM((width, count), jnp.float32),
            pltpu.VMEM((3, heads, HEAD, width), jnp.bfloat16),
            pltpu.SemaphoreType.DMA((3,)),
        ],
        compiler_params=pltpu.CompilerParams(vmem_limit_bytes=VMEM_LIMIT),
        cost_estimate=pl.CostEstimate(
            flops=10 * count * width * width, bytes_accessed=10 * 2**20, transcendentals=0
        ),
        name="finish",
    )(*args)


def scan_kernel(coefs, first, everyone, out):
    running = first[...].astype(jnp.float32)
    for step in range(everyone.shape[0]):
        running = running + coefs[step] * everyone[step].astype(jnp.float32)
        out[step] = running.astype(jnp.bfloat16)


def scan(coefs, first, everyone):
    return pl.pallas_call(
        scan_kernel,
        grid_spec=pltpu.PrefetchScalarGridSpec(
            num_scalar_prefetch=1,
            grid=(),
            in_specs=[pl.BlockSpec(memory_space=pltpu.VMEM)] * 2,
            out_specs=pl.BlockSpec(memory_space=pltpu.VMEM),
        ),
        out_shape=jax.ShapeDtypeStruct(everyone.shape, jnp.bfloat16),
        compiler_params=pltpu.CompilerParams(vmem_limit_bytes=16 * 2**20),
        name="scan",
    )(coefs, first, everyone)


def body(latents, timesteps, experts, offset, modulation, coef, w_qkv, w_o, w_cq, w_co, text_kv):
    step_index = lax.axis_index("step")
    steps = lax.axis_size("step")
    position = offset[0] + step_index
    entry = lax.dynamic_index_in_dim(timesteps, position, 0, False)
    expert = lax.dynamic_index_in_dim(experts, position, 0, False)
    modulate = lax.dynamic_index_in_dim(modulation, entry, 0, False)
    latent = latents[0]
    count, width = latent.shape
    heads = width // HEAD
    normed = norm(latent, jnp.swapaxes(modulation, 0, 1), entry[None])
    own_qkv = lax.dynamic_index_in_dim(w_qkv, expert, 0, False)[:, 0, :]
    w_mixed = jnp.pad(own_qkv, ((0, 0), (0, 2 * LANES - 3 * HEAD)))

    def over_steps(value):
        shaped = value.reshape(steps, -1, width)
        return lax.all_to_all(shaped, "step", split_axis=0, concat_axis=0, tiled=True)

    first = over_steps(latent)[0]
    own_text = lax.dynamic_index_in_dim(text_kv, expert, 0, False).reshape(2, TEXT, heads, HEAD)
    text_keys = jnp.pad(
        jnp.transpose(own_text[0], (1, 0, 2)), ((0, 0), (0, TEXT_PAD - TEXT), (0, 0))
    )
    text_values = jnp.pad(
        jnp.transpose(own_text[1], (1, 2, 0)), ((0, 0), (0, 0), (0, TEXT_PAD - TEXT))
    )
    first, text_keys, text_values = link([first, text_keys, text_values], [])
    own_weights = jnp.stack(
        [
            lax.dynamic_index_in_dim(w_o, expert, 0, False),
            jnp.swapaxes(lax.dynamic_index_in_dim(w_cq, expert, 0, False), 0, 1),
            lax.dynamic_index_in_dim(w_co, expert, 0, False),
        ]
    )
    heads_out, chunks = self_attend(
        normed, w_mixed, ([], [first, text_keys, text_values, own_weights, w_mixed])
    )
    all_weights = lax.all_gather(
        link([own_weights], [chunks[0][0]])[0], "tok", axis=0, tiled=False
    )

    def returned(value):
        back = lax.all_to_all(value, "tok", split_axis=0, concat_axis=0, tiled=True)
        return back.reshape(width, -1)

    turned = [returned(heads_out[0])]
    turned.append(returned(link([heads_out[1]], [turned[0], all_weights])[0]))
    predicted = finish(turned, latent, modulate[2][None], all_weights, text_keys, text_values)
    coefs = jnp.take(coef, lax.dynamic_slice_in_dim(timesteps, offset[0], steps))
    return over_steps(scan(coefs, first, over_steps(predicted))).reshape(1, count, width)


def solution(mesh):
    in_specs = (
        P("step", "tok", None),
        P(),
        P(),
        P(),
        P(),
        P(),
        P(None, None, "tok", None),
        P(None, "tok", None),
        P(None, None, "tok"),
        P(None, "tok", None),
        P(),
    )
    out_specs = P("step", "tok", None)
    return jax.shard_map(body, mesh=mesh, in_specs=in_specs, out_specs=out_specs, check_vma=False)
```

```python
import functools
import math

import jax
import jax.numpy as jnp
from jax import lax
from jax.experimental import pallas as pl
from jax.experimental.pallas import tpu as pltpu
from jax.sharding import PartitionSpec as P

HEAD = 72
LANES = 128
TEXT = 300
TEXT_PAD = 384
CHUNKS = (384, 128)
SOURCES = (2, 8)
ROW_BLOCK = 1024
ROWS = 128
KEY_BLOCK = 1024
HALVES = 2
VALUE = 2 * HEAD - LANES
FACTOR = math.log2(math.e) / HEAD**0.5
VMEM_LIMIT = 60 * 2**20
HELD = ((0, 0), (-1, 0), (1, 0), (0, 1), (-1, 1), (1, 1), (2, 0), (2, 1))


def place(y, x, core):
    return (y % 4) * 4 + x * 2 + core


def moved(value, dy, dx, dcore):
    perm = [
        (place(y, x, core), place(y + dy, x ^ dx, core ^ dcore))
        for y in range(4)
        for x in range(2)
        for core in range(2)
    ]
    return lax.ppermute(value, "tok", perm)


def gather_near(own):
    half = own.shape[0] // 2
    above, below, across = moved(own, 1, 0, 0), moved(own, -1, 0, 0), moved(own, 0, 1, 0)
    return (
        own,
        above,
        below,
        across,
        moved(above, 0, 1, 0),
        moved(across, -1, 0, 0),
        moved(above, 1, 0, 0),
        moved(above[:half], 1, 1, 0),
        moved(below[half:], -1, 1, 0),
    )


def link_kernel(passed, *refs):
    del passed, refs


def link(values, after):
    values = list(values)
    return pl.pallas_call(
        functools.partial(link_kernel, len(values)),
        in_specs=[pl.BlockSpec(memory_space=pl.ANY)] * (len(values) + len(after)),
        out_specs=[pl.BlockSpec(memory_space=pl.ANY)] * len(values),
        out_shape=[jax.ShapeDtypeStruct(value.shape, value.dtype) for value in values],
        input_output_aliases={index: index for index in range(len(values))},
        compiler_params=pltpu.CompilerParams(vmem_limit_bytes=VMEM_LIMIT),
        name="link",
    )(*values, *after)


def whole(array):
    return pl.BlockSpec(array.shape, lambda *_: (0,) * len(array.shape))


def norm_kernel(entry, latent, modulation, *outs):
    flat = latent[...].astype(jnp.float32)
    mean = jnp.mean(flat, axis=1, keepdims=True)
    centred = flat - mean
    var = jnp.mean(centred**2, axis=1, keepdims=True)
    row = pl.ds(entry[0] % 8, 1)
    shift, scale = modulation[0, row, :], modulation[1, row, :]
    normed = (centred * lax.rsqrt(var + 1e-06) * (1.0 + scale) + shift).astype(jnp.bfloat16)
    here = pl.program_id(0)
    first = CHUNKS[0] // ROWS

    @pl.when(here < first)
    def _():
        outs[0][...] = normed

    @pl.when(here >= first)
    def _():
        outs[1][...] = normed


def norm(latent, modulation, entry):
    count, width = latent.shape
    first = CHUNKS[0] // ROWS
    block = (ROWS, width)
    return pl.pallas_call(
        norm_kernel,
        grid_spec=pltpu.PrefetchScalarGridSpec(
            num_scalar_prefetch=1,
            grid=(count // ROWS,),
            in_specs=[
                pl.BlockSpec(block, lambda i, entry: (i, 0)),
                pl.BlockSpec((3, 8, width), lambda i, entry: (0, entry[0] // 8, 0)),
            ],
            out_specs=[
                pl.BlockSpec(block, lambda i, entry: (jnp.minimum(i, first - 1), 0)),
                pl.BlockSpec(block, lambda i, entry: (jnp.maximum(i - first, 0), 0)),
            ],
        ),
        out_shape=[jax.ShapeDtypeStruct((per, width), jnp.bfloat16) for per in CHUNKS],
        compiler_params=pltpu.CompilerParams(vmem_limit_bytes=VMEM_LIMIT),
        name="norm",
    )(entry, latent, modulation)


def split_heads(mixed, queries, keys, values):
    low, high = mixed[:, :LANES], mixed[:, LANES:]
    queries[...] = low.astype(jnp.bfloat16)
    lane = lax.broadcasted_iota(jnp.int32, high.shape, 1)
    values[...] = jnp.where(lane >= VALUE + HEAD, 1.0, high).astype(jnp.bfloat16)
    pad = jnp.zeros((LANES - HEAD, mixed.shape[0]), jnp.float32)
    keys[...] = jnp.concatenate([low.T[HEAD:], high.T[:VALUE], pad], 0).astype(jnp.bfloat16)


def project_kernel(waited, *refs):
    rows, weights, queries, keys, values = refs[waited:]
    mixed = jnp.dot(rows[...], weights[...], preferred_element_type=jnp.float32)
    split_heads(mixed, queries, keys, values)


def project_near_kernel(*refs):
    blocks, weights, outs, rows = refs[:-8], refs[-8], refs[-7:-1], refs[-1]
    start = 0
    for block in blocks:
        rows[start : start + block.shape[0], :] = block[...]
        start += block.shape[0]
    mixed = jnp.dot(rows[...], weights[...], preferred_element_type=jnp.float32)
    split_heads(mixed[:, : 2 * LANES], *outs[:3])
    split_heads(mixed[:, 2 * LANES :], *outs[3:])


def project_near(blocks, weights):
    count = sum(block.shape[0] for block in blocks)
    width = weights.shape[0]
    flat = jax.ShapeDtypeStruct((count, LANES), jnp.bfloat16)
    turned = jax.ShapeDtypeStruct((LANES, count), jnp.bfloat16)
    outs = [flat, turned, flat] * 2
    results = pl.pallas_call(
        project_near_kernel,
        grid=(1,),
        in_specs=[whole(arg) for arg in (*blocks, weights)],
        out_specs=[whole(out) for out in outs],
        out_shape=outs,
        scratch_shapes=[pltpu.VMEM((count, width), jnp.bfloat16)],
        compiler_params=pltpu.CompilerParams(vmem_limit_bytes=VMEM_LIMIT),
        cost_estimate=pl.CostEstimate(
            flops=8 * count * width * LANES,
            bytes_accessed=count * width * 2 + count * 12 * LANES,
            transcendentals=0,
        ),
        name="project_near",
    )(*blocks, weights)
    return results[:3], results[3:]


def project(tokens, weights, after):
    count, width = tokens.shape
    flat = jax.ShapeDtypeStruct((count, LANES), jnp.bfloat16)
    turned = jax.ShapeDtypeStruct((LANES, count), jnp.bfloat16)
    flat_spec = pl.BlockSpec((ROW_BLOCK, LANES), lambda i: (i, 0))
    return pl.pallas_call(
        functools.partial(project_kernel, len(after)),
        grid=(count // ROW_BLOCK,),
        in_specs=[pl.BlockSpec(memory_space=pl.ANY)] * len(after)
        + [pl.BlockSpec((ROW_BLOCK, width), lambda i: (i, 0)), whole(weights)],
        out_specs=[flat_spec, pl.BlockSpec((LANES, ROW_BLOCK), lambda i: (0, i)), flat_spec],
        out_shape=(flat, turned, flat),
        compiler_params=pltpu.CompilerParams(vmem_limit_bytes=VMEM_LIMIT),
        cost_estimate=pl.CostEstimate(
            flops=4 * count * width * LANES,
            bytes_accessed=count * width * 2 + count * 6 * LANES,
            transcendentals=0,
        ),
        name="project",
    )(*after, tokens, weights)


def attend_kernel(waited, key_chunks, carried, final, order, *refs):
    refs = list(refs)[waited:]
    query_ref = refs.pop(0)
    keys = refs[:key_chunks]
    values = refs[key_chunks : 2 * key_chunks]
    del refs[: 2 * key_chunks]
    state = refs.pop(0) if carried else None
    out, scores = refs
    parts = [
        (key, value, slice(start, start + KEY_BLOCK))
        for key, value in zip(keys, values)
        for start in range(0, key.shape[1], KEY_BLOCK)
    ]
    rows = query_ref.shape[0] // HALVES
    spans = [slice(half * rows, (half + 1) * rows) for half in range(HALVES)]
    units = [(half, step) for step in range(len(parts)) for half in range(HALVES)]

    def score(unit):
        half, step = unit
        key, _, span = parts[step]
        return jnp.dot(
            query_ref[spans[half], :], key[:, span], preferred_element_type=jnp.float32
        )

    totals = [state[span, :] if carried else None for span in spans]
    tops = [total[:, LANES - 1 :] if carried else None for total in totals]
    scores[0] = score(units[0])
    for index, (half, step) in enumerate(units):
        if index + 1 < len(units):
            scores[(index + 1) % 2] = score(units[index + 1])
        now = scores[index % 2]
        top, total = tops[half], totals[half]
        high = jnp.max(now, axis=1, keepdims=True)
        newer = high if top is None else jnp.maximum(top, high)
        weights = jnp.exp2(now * FACTOR - newer * FACTOR).astype(jnp.bfloat16)
        _, value, span = parts[step]
        part = jnp.dot(weights, value[span, :], preferred_element_type=jnp.float32)
        totals[half] = part if top is None else total * jnp.exp2((top - newer) * FACTOR) + part
        tops[half] = newer
    for half, (total, top) in enumerate(zip(totals, tops)):
        if final:
            turned = total.T
            done = turned[VALUE : VALUE + HEAD] / turned[VALUE + HEAD : VALUE + HEAD + 1]
            per = out.shape[2]
            first = pl.program_id(0) * (HALVES * rows // per) + half * (rows // per)
            for piece in range(rows // per):
                out[order[first + piece]] = done[:, piece * per : (piece + 1) * per].astype(
                    jnp.bfloat16
                )
        else:
            lane = lax.broadcasted_iota(jnp.int32, total.shape, 1)
            out[spans[half], :] = jnp.where(lane == LANES - 1, top, total)


def attend_chunk(queries, per, together, sources, state, order, after):
    count = queries.shape[0]
    block = per * together
    row_spec = pl.BlockSpec((block, LANES), lambda i, o: (i, 0))
    args = [*after, queries]
    in_specs = [pl.BlockSpec(memory_space=pl.ANY)] * len(after) + [row_spec]
    for index in (1, 2):
        args += [chunk[index] for chunk in sources]
        in_specs += [whole(chunk[index]) for chunk in sources]
    if state is not None:
        args.append(state)
        in_specs.append(row_spec)
    final = order is not None
    if final:
        out_shape = jax.ShapeDtypeStruct((count // per, HEAD, per), jnp.bfloat16)
        out_spec = whole(out_shape)
    else:
        order = jnp.arange(count // per, dtype=jnp.int32)
        out_shape = jax.ShapeDtypeStruct((count, LANES), jnp.float32)
        out_spec = row_spec
    pairs = count * sum(chunk[1].shape[1] for chunk in sources)
    return pl.pallas_call(
        functools.partial(attend_kernel, len(after), len(sources), state is not None, final),
        grid_spec=pltpu.PrefetchScalarGridSpec(
            num_scalar_prefetch=1,
            grid=(count // block,),
            in_specs=in_specs,
            out_specs=out_spec,
            scratch_shapes=[pltpu.VMEM((2, block // HALVES, KEY_BLOCK), jnp.float32)],
        ),
        out_shape=out_shape,
        compiler_params=pltpu.CompilerParams(vmem_limit_bytes=VMEM_LIMIT),
        cost_estimate=pl.CostEstimate(
            flops=4 * pairs * LANES * 2, bytes_accessed=4 * 2**20, transcendentals=pairs
        ),
        name="self_attend",
    )(order, *args)


def self_attend(normed, own_weights, both_weights, order, early):
    gathered = lax.all_gather(normed[0], "tok", axis=0, tiled=True)
    own, other = project_near(gather_near(normed[1]), both_weights)
    part = [moved(value, 0, 0, 1) for value in other]
    near = jnp.concatenate([own[0], part[0]], 0)
    state = attend_chunk(near, CHUNKS[1], SOURCES[1], [own, part], None, None, early)
    far = project(gathered, own_weights, [state])
    everyone = jnp.arange(order.shape[0], dtype=jnp.int32)
    far_out = attend_chunk(far[0], CHUNKS[0], SOURCES[0], [own, part, far], None, everyone, [])
    near_out = attend_chunk(near, CHUNKS[1], SOURCES[1], [far], state, order, [far_out])
    return [far_out, near_out], far


def finish_kernel(parts, *refs):
    turned, (latent, gate, weights, keys, values) = refs[:parts], refs[parts : parts + 5]
    out, cross, near, arrived = refs[parts + 5 :]
    width = latent.shape[1]
    copies = [
        pltpu.make_async_copy(weights.at[:, index], near.at[index], arrived.at[index])
        for index in range(3)
    ]
    for copy in copies:
        copy.start()

    def weight(index):
        copies[index].wait()
        return near[index].astype(jnp.float32).reshape(width, width).astype(jnp.bfloat16)

    attended = jnp.concatenate([part[...].astype(jnp.float32) for part in turned], 1)
    attended = attended.T.astype(jnp.bfloat16)
    projected = jnp.dot(attended, weight(0), preferred_element_type=jnp.float32)
    hidden = (latent[...].astype(jnp.float32) + gate[...] * projected).astype(jnp.bfloat16)
    queries = lax.dot_general(
        weight(1), hidden, (((1,), (1,)), ((), ())), preferred_element_type=jnp.float32
    )
    for head in range(width // HEAD):
        rows = slice(head * HEAD, (head + 1) * HEAD)
        scores = jnp.dot(
            keys[head], queries[rows].astype(jnp.bfloat16), preferred_element_type=jnp.float32
        )
        row = lax.broadcasted_iota(jnp.int32, scores.shape, 0)
        scores = jnp.where(row < TEXT, scores, -jnp.inf)
        high = jnp.max(scores, axis=0, keepdims=True)
        exps = jnp.exp2((scores - high) * FACTOR)
        total = jnp.sum(exps, axis=0, keepdims=True)
        result = jnp.dot(
            values[head], exps.astype(jnp.bfloat16), preferred_element_type=jnp.float32
        )
        cross[rows, :] = result / total
    crossed = cross[...].T.astype(jnp.bfloat16)
    out[...] = (
        hidden.astype(jnp.float32)
        + jnp.dot(crossed, weight(2), preferred_element_type=jnp.float32)
    ).astype(jnp.bfloat16)


def finish(turned, latent, gate, weights, keys, values):
    count, width = latent.shape
    heads = width // HEAD
    args = (*turned, latent, gate, weights, keys, values)
    return pl.pallas_call(
        functools.partial(finish_kernel, len(turned)),
        grid=(1,),
        in_specs=[
            pl.BlockSpec(memory_space=pl.ANY) if arg is weights else whole(arg) for arg in args
        ],
        out_specs=whole(latent),
        out_shape=jax.ShapeDtypeStruct((count, width), jnp.bfloat16),
        scratch_shapes=[
            pltpu.VMEM((width, count), jnp.float32),
            pltpu.VMEM((3, heads, HEAD, width), jnp.bfloat16),
            pltpu.SemaphoreType.DMA((3,)),
        ],
        compiler_params=pltpu.CompilerParams(vmem_limit_bytes=VMEM_LIMIT),
        cost_estimate=pl.CostEstimate(
            flops=10 * count * width * width, bytes_accessed=10 * 2**20, transcendentals=0
        ),
        name="finish",
    )(*args)


def scan_kernel(coefs, first, everyone, out):
    running = first[...].astype(jnp.float32)
    for step in range(everyone.shape[0]):
        running = running + coefs[step] * everyone[step].astype(jnp.float32)
        out[step] = running.astype(jnp.bfloat16)


def scan(coefs, first, everyone):
    return pl.pallas_call(
        scan_kernel,
        grid_spec=pltpu.PrefetchScalarGridSpec(
            num_scalar_prefetch=1,
            grid=(),
            in_specs=[pl.BlockSpec(memory_space=pltpu.VMEM)] * 2,
            out_specs=pl.BlockSpec(memory_space=pltpu.VMEM),
        ),
        out_shape=jax.ShapeDtypeStruct(everyone.shape, jnp.bfloat16),
        compiler_params=pltpu.CompilerParams(vmem_limit_bytes=16 * 2**20),
        name="scan",
    )(coefs, first, everyone)


def body(latents, timesteps, experts, offset, modulation, coef, w_qkv, w_o, w_cq, w_co, text_kv):
    step_index = lax.axis_index("step")
    steps = lax.axis_size("step")
    position = offset[0] + step_index
    entry = lax.dynamic_index_in_dim(timesteps, position, 0, False)
    expert = lax.dynamic_index_in_dim(experts, position, 0, False)
    modulate = lax.dynamic_index_in_dim(modulation, entry, 0, False)
    latent = latents[0]
    count, width = latent.shape
    heads = width // HEAD
    normed = norm(latent, jnp.swapaxes(modulation, 0, 1), entry[None])
    own_qkv = lax.dynamic_index_in_dim(w_qkv, expert, 0, False)[:, 0, :]
    w_mixed = jnp.pad(own_qkv, ((0, 0), (0, 2 * LANES - 3 * HEAD)))

    def over_steps(value):
        shaped = value.reshape(steps, -1, width)
        return lax.all_to_all(shaped, "step", split_axis=0, concat_axis=0, tiled=True)

    first = over_steps(latent)[0]
    own_text = lax.dynamic_index_in_dim(text_kv, expert, 0, False).reshape(2, TEXT, heads, HEAD)
    text_keys = jnp.pad(
        jnp.transpose(own_text[0], (1, 0, 2)), ((0, 0), (0, TEXT_PAD - TEXT), (0, 0))
    )
    text_values = jnp.pad(
        jnp.transpose(own_text[1], (1, 2, 0)), ((0, 0), (0, 0), (0, TEXT_PAD - TEXT))
    )
    first, text_keys, text_values = link([first, text_keys, text_values], [])
    own_weights = jnp.stack(
        [
            lax.dynamic_index_in_dim(w_o, expert, 0, False),
            jnp.swapaxes(lax.dynamic_index_in_dim(w_cq, expert, 0, False), 0, 1),
            lax.dynamic_index_in_dim(w_co, expert, 0, False),
        ]
    )
    w_both = jnp.concatenate([w_mixed, moved(w_mixed, 0, 0, 1)], 1)
    me = lax.axis_index("tok")
    y, x, core = me // 4, me // 2 % 2, me % 2
    order = jnp.stack(
        [place(y + dy + 4, x ^ dx, core ^ dcore) for dcore in range(2) for dy, dx in HELD]
    ).astype(jnp.int32)
    heads_out, far = self_attend(
        normed, w_mixed, w_both, order, [first, text_keys, text_values, own_weights]
    )
    all_weights = lax.all_gather(
        link([own_weights], [far[0]])[0], "tok", axis=0, tiled=False
    )

    def returned(value):
        back = lax.all_to_all(value, "tok", split_axis=0, concat_axis=0, tiled=True)
        return back.reshape(width, -1)

    turned = [returned(heads_out[0])]
    turned.append(returned(link([heads_out[1]], [turned[0], all_weights])[0]))
    predicted = finish(turned, latent, modulate[2][None], all_weights, text_keys, text_values)
    coefs = jnp.take(coef, lax.dynamic_slice_in_dim(timesteps, offset[0], steps))
    return over_steps(scan(coefs, first, over_steps(predicted))).reshape(1, count, width)


def solution(mesh):
    in_specs = (
        P("step", "tok", None),
        P(),
        P(),
        P(),
        P(),
        P(),
        P(None, None, "tok", None),
        P(None, "tok", None),
        P(None, None, "tok"),
        P(None, "tok", None),
        P(),
    )
    out_specs = P("step", "tok", None)
    return jax.shard_map(body, mesh=mesh, in_specs=in_specs, out_specs=out_specs, check_vma=False)
```

```python
import functools
import math

import jax
import jax.numpy as jnp
from jax import lax
from jax.experimental import pallas as pl
from jax.experimental.pallas import tpu as pltpu
from jax.sharding import PartitionSpec as P

HEAD = 72
LANES = 128
TEXT = 300
TEXT_PAD = 384
CHUNKS = (384, 128)
SOURCES = (4, 8)
ROW_BLOCK = 1024
ROWS = 128
KEY_BLOCK = 1024
HALVES = 2
VALUE = 2 * HEAD - LANES
FACTOR = math.log2(math.e) / HEAD**0.5
VMEM_LIMIT = 60 * 2**20
def link_kernel(passed, *refs):
    del passed, refs


def link(values, after):
    values = list(values)
    return pl.pallas_call(
        functools.partial(link_kernel, len(values)),
        in_specs=[pl.BlockSpec(memory_space=pl.ANY)] * (len(values) + len(after)),
        out_specs=[pl.BlockSpec(memory_space=pl.ANY)] * len(values),
        out_shape=[jax.ShapeDtypeStruct(value.shape, value.dtype) for value in values],
        input_output_aliases={index: index for index in range(len(values))},
        compiler_params=pltpu.CompilerParams(vmem_limit_bytes=VMEM_LIMIT),
        name="link",
    )(*values, *after)


def whole(array):
    return pl.BlockSpec(array.shape, lambda *_: (0,) * len(array.shape))


def norm_kernel(entry, latent, modulation, *outs):
    flat = latent[...].astype(jnp.float32)
    mean = jnp.mean(flat, axis=1, keepdims=True)
    centred = flat - mean
    var = jnp.mean(centred**2, axis=1, keepdims=True)
    row = pl.ds(entry[0] % 8, 1)
    shift, scale = modulation[0, row, :], modulation[1, row, :]
    normed = (centred * lax.rsqrt(var + 1e-06) * (1.0 + scale) + shift).astype(jnp.bfloat16)
    here = pl.program_id(0)
    first = CHUNKS[0] // ROWS

    @pl.when(here < first)
    def _():
        outs[0][...] = normed

    @pl.when(here >= first)
    def _():
        outs[1][...] = normed


def norm(latent, modulation, entry):
    count, width = latent.shape
    first = CHUNKS[0] // ROWS
    block = (ROWS, width)
    return pl.pallas_call(
        norm_kernel,
        grid_spec=pltpu.PrefetchScalarGridSpec(
            num_scalar_prefetch=1,
            grid=(count // ROWS,),
            in_specs=[
                pl.BlockSpec(block, lambda i, entry: (i, 0)),
                pl.BlockSpec((3, 8, width), lambda i, entry: (0, entry[0] // 8, 0)),
            ],
            out_specs=[
                pl.BlockSpec(block, lambda i, entry: (jnp.minimum(i, first - 1), 0)),
                pl.BlockSpec(block, lambda i, entry: (jnp.maximum(i - first, 0), 0)),
            ],
        ),
        out_shape=[jax.ShapeDtypeStruct((per, width), jnp.bfloat16) for per in CHUNKS],
        compiler_params=pltpu.CompilerParams(vmem_limit_bytes=VMEM_LIMIT),
        name="norm",
    )(entry, latent, modulation)


def project_kernel(waited, *refs):
    rows, weights, queries, keys, values = refs[waited:]
    mixed = jnp.dot(rows[...], weights[...], preferred_element_type=jnp.float32)
    low, high = mixed[:, :LANES], mixed[:, LANES:]
    queries[...] = low.astype(jnp.bfloat16)
    lane = lax.broadcasted_iota(jnp.int32, high.shape, 1)
    values[...] = jnp.where(lane >= VALUE + HEAD, 1.0, high).astype(jnp.bfloat16)
    pad = jnp.zeros((LANES - HEAD, mixed.shape[0]), jnp.float32)
    keys[...] = jnp.concatenate([low.T[HEAD:], high.T[:VALUE], pad], 0).astype(jnp.bfloat16)


def project(tokens, weights, after):
    count, width = tokens.shape
    flat = jax.ShapeDtypeStruct((count, LANES), jnp.bfloat16)
    turned = jax.ShapeDtypeStruct((LANES, count), jnp.bfloat16)
    flat_spec = pl.BlockSpec((ROW_BLOCK, LANES), lambda i: (i, 0))
    return pl.pallas_call(
        functools.partial(project_kernel, len(after)),
        grid=(count // ROW_BLOCK,),
        in_specs=[pl.BlockSpec(memory_space=pl.ANY)] * len(after)
        + [pl.BlockSpec((ROW_BLOCK, width), lambda i: (i, 0)), whole(weights)],
        out_specs=[flat_spec, pl.BlockSpec((LANES, ROW_BLOCK), lambda i: (0, i)), flat_spec],
        out_shape=(flat, turned, flat),
        compiler_params=pltpu.CompilerParams(vmem_limit_bytes=VMEM_LIMIT),
        cost_estimate=pl.CostEstimate(
            flops=4 * count * width * LANES,
            bytes_accessed=count * width * 2 + count * 6 * LANES,
            transcendentals=0,
        ),
        name="project",
    )(*after, tokens, weights)


def attend_kernel(waited, key_chunks, carried, final, *refs):
    refs = list(refs)[waited:]
    query_ref = refs.pop(0)
    keys = refs[:key_chunks]
    values = refs[key_chunks : 2 * key_chunks]
    del refs[: 2 * key_chunks]
    state = refs.pop(0) if carried else None
    out, scores = refs
    parts = [
        (key, value, slice(start, start + KEY_BLOCK))
        for key, value in zip(keys, values)
        for start in range(0, key.shape[1], KEY_BLOCK)
    ]
    rows = query_ref.shape[0] // HALVES
    spans = [slice(half * rows, (half + 1) * rows) for half in range(HALVES)]
    units = [(half, step) for step in range(len(parts)) for half in range(HALVES)]

    def score(unit):
        half, step = unit
        key, _, span = parts[step]
        return jnp.dot(
            query_ref[spans[half], :], key[:, span], preferred_element_type=jnp.float32
        )

    totals = [state[span, :] if carried else None for span in spans]
    tops = [total[:, LANES - 1 :] if carried else None for total in totals]
    scores[0] = score(units[0])
    for index, (half, step) in enumerate(units):
        if index + 1 < len(units):
            scores[(index + 1) % 2] = score(units[index + 1])
        now = scores[index % 2]
        top, total = tops[half], totals[half]
        high = jnp.max(now, axis=1, keepdims=True)
        newer = high if top is None else jnp.maximum(top, high)
        weights = jnp.exp2(now * FACTOR - newer * FACTOR).astype(jnp.bfloat16)
        _, value, span = parts[step]
        part = jnp.dot(weights, value[span, :], preferred_element_type=jnp.float32)
        totals[half] = part if top is None else total * jnp.exp2((top - newer) * FACTOR) + part
        tops[half] = newer
    for half, (total, top) in enumerate(zip(totals, tops)):
        if final:
            turned = total.T
            done = turned[VALUE : VALUE + HEAD] / turned[VALUE + HEAD : VALUE + HEAD + 1]
            per = out.shape[2]
            for piece in range(rows // per):
                out[half * (rows // per) + piece] = done[
                    :, piece * per : (piece + 1) * per
                ].astype(jnp.bfloat16)
        else:
            lane = lax.broadcasted_iota(jnp.int32, total.shape, 1)
            out[spans[half], :] = jnp.where(lane == LANES - 1, top, total)


def attend_chunk(queries, per, together, sources, state, final, after):
    count = queries.shape[0]
    block = per * together
    row_spec = pl.BlockSpec((block, LANES), lambda i: (i, 0))
    args = [*after, queries]
    in_specs = [pl.BlockSpec(memory_space=pl.ANY)] * len(after) + [row_spec]
    for index in (1, 2):
        args += [chunk[index] for chunk in sources]
        in_specs += [whole(chunk[index]) for chunk in sources]
    if state is not None:
        args.append(state)
        in_specs.append(row_spec)
    if final:
        out_shape = jax.ShapeDtypeStruct((count // per, HEAD, per), jnp.bfloat16)
        out_spec = pl.BlockSpec((together, HEAD, per), lambda i: (i, 0, 0))
    else:
        out_shape = jax.ShapeDtypeStruct((count, LANES), jnp.float32)
        out_spec = row_spec
    pairs = count * sum(chunk[1].shape[1] for chunk in sources)
    return pl.pallas_call(
        functools.partial(attend_kernel, len(after), len(sources), state is not None, final),
        grid=(count // block,),
        in_specs=in_specs,
        out_specs=out_spec,
        scratch_shapes=[
            pltpu.VMEM((2, block // HALVES, KEY_BLOCK), jnp.float32),
        ],
        out_shape=out_shape,
        compiler_params=pltpu.CompilerParams(vmem_limit_bytes=VMEM_LIMIT),
        cost_estimate=pl.CostEstimate(
            flops=4 * pairs * LANES * 2, bytes_accessed=4 * 2**20, transcendentals=pairs
        ),
        name="self_attend",
    )(*args)


def self_attend(normed, weights, early):
    chunks, states, previous = [], [], []
    held = None
    for chunk in range(len(CHUNKS)):
        own = normed[chunk]
        if held is not None:
            own = link([own], [held] + early[chunk])[0]
        held = lax.all_gather(own, "tok", axis=0, tiled=True)
        chunks.append([held])
    for chunk in range(len(CHUNKS)):
        last = chunk + 1 == len(CHUNKS)
        chunks[chunk] = project(chunks[chunk][0], weights, previous)
        for earlier in range(chunk + 1):
            before = states[earlier] if earlier < chunk else None
            keys = chunks[chunk : chunk + 1] if earlier < chunk else chunks[: chunk + 1]
            result = attend_chunk(
                chunks[earlier][0], CHUNKS[earlier], SOURCES[earlier], keys, before, last, previous
            )
            previous = [result]
            states[earlier : earlier + 1] = [result]
    return states, chunks


def finish_kernel(parts, *refs):
    turned, (latent, gate, weights, keys, values) = refs[:parts], refs[parts : parts + 5]
    out, cross, near, arrived = refs[parts + 5 :]
    width = latent.shape[1]
    copies = [
        pltpu.make_async_copy(weights.at[:, index], near.at[index], arrived.at[index])
        for index in range(3)
    ]
    for copy in copies:
        copy.start()

    def weight(index):
        copies[index].wait()
        return near[index].astype(jnp.float32).reshape(width, width).astype(jnp.bfloat16)

    attended = jnp.concatenate([part[...].astype(jnp.float32) for part in turned], 1)
    attended = attended.T.astype(jnp.bfloat16)
    projected = jnp.dot(attended, weight(0), preferred_element_type=jnp.float32)
    hidden = (latent[...].astype(jnp.float32) + gate[...] * projected).astype(jnp.bfloat16)
    queries = lax.dot_general(
        weight(1), hidden, (((1,), (1,)), ((), ())), preferred_element_type=jnp.float32
    )
    for head in range(width // HEAD):
        rows = slice(head * HEAD, (head + 1) * HEAD)
        scores = jnp.dot(
            keys[head], queries[rows].astype(jnp.bfloat16), preferred_element_type=jnp.float32
        )
        row = lax.broadcasted_iota(jnp.int32, scores.shape, 0)
        scores = jnp.where(row < TEXT, scores, -jnp.inf)
        high = jnp.max(scores, axis=0, keepdims=True)
        exps = jnp.exp2((scores - high) * FACTOR)
        total = jnp.sum(exps, axis=0, keepdims=True)
        result = jnp.dot(
            values[head], exps.astype(jnp.bfloat16), preferred_element_type=jnp.float32
        )
        cross[rows, :] = result / total
    crossed = cross[...].T.astype(jnp.bfloat16)
    out[...] = (
        hidden.astype(jnp.float32)
        + jnp.dot(crossed, weight(2), preferred_element_type=jnp.float32)
    ).astype(jnp.bfloat16)


def finish(turned, latent, gate, weights, keys, values):
    count, width = latent.shape
    heads = width // HEAD
    args = (*turned, latent, gate, weights, keys, values)
    return pl.pallas_call(
        functools.partial(finish_kernel, len(turned)),
        grid=(1,),
        in_specs=[
            pl.BlockSpec(memory_space=pl.ANY) if arg is weights else whole(arg) for arg in args
        ],
        out_specs=whole(latent),
        out_shape=jax.ShapeDtypeStruct((count, width), jnp.bfloat16),
        scratch_shapes=[
            pltpu.VMEM((width, count), jnp.float32),
            pltpu.VMEM((3, heads, HEAD, width), jnp.bfloat16),
            pltpu.SemaphoreType.DMA((3,)),
        ],
        compiler_params=pltpu.CompilerParams(vmem_limit_bytes=VMEM_LIMIT),
        cost_estimate=pl.CostEstimate(
            flops=10 * count * width * width, bytes_accessed=10 * 2**20, transcendentals=0
        ),
        name="finish",
    )(*args)


def scan_kernel(coefs, first, everyone, out):
    running = first[...].astype(jnp.float32)
    for step in range(everyone.shape[0]):
        running = running + coefs[step] * everyone[step].astype(jnp.float32)
        out[step] = running.astype(jnp.bfloat16)


def scan(coefs, first, everyone):
    return pl.pallas_call(
        scan_kernel,
        grid_spec=pltpu.PrefetchScalarGridSpec(
            num_scalar_prefetch=1,
            grid=(),
            in_specs=[pl.BlockSpec(memory_space=pltpu.VMEM)] * 2,
            out_specs=pl.BlockSpec(memory_space=pltpu.VMEM),
        ),
        out_shape=jax.ShapeDtypeStruct(everyone.shape, jnp.bfloat16),
        compiler_params=pltpu.CompilerParams(vmem_limit_bytes=16 * 2**20),
        name="scan",
    )(coefs, first, everyone)


def body(latents, timesteps, experts, offset, modulation, coef, w_qkv, w_o, w_cq, w_co, text_kv):
    step_index = lax.axis_index("step")
    steps = lax.axis_size("step")
    position = offset[0] + step_index
    entry = lax.dynamic_index_in_dim(timesteps, position, 0, False)
    expert = lax.dynamic_index_in_dim(experts, position, 0, False)
    modulate = lax.dynamic_index_in_dim(modulation, entry, 0, False)
    latent = latents[0]
    count, width = latent.shape
    heads = width // HEAD
    normed = norm(latent, jnp.swapaxes(modulation, 0, 1), entry[None])
    own_qkv = lax.dynamic_index_in_dim(w_qkv, expert, 0, False)[:, 0, :]
    w_mixed = jnp.pad(own_qkv, ((0, 0), (0, 2 * LANES - 3 * HEAD)))

    def over_steps(value):
        shaped = value.reshape(steps, -1, width)
        return lax.all_to_all(shaped, "step", split_axis=0, concat_axis=0, tiled=True)

    shares = latent.reshape(steps, -1, width)
    first = jnp.where(step_index == 0, shares[0], jnp.zeros_like(shares[0]))
    for step in range(1, steps):
        first = first + lax.ppermute(shares[step], "step", [(0, step)])
    own_text = lax.dynamic_index_in_dim(text_kv, expert, 0, False).reshape(2, TEXT, heads, HEAD)
    text_keys = jnp.pad(
        jnp.transpose(own_text[0], (1, 0, 2)), ((0, 0), (0, TEXT_PAD - TEXT), (0, 0))
    )
    text_values = jnp.pad(
        jnp.transpose(own_text[1], (1, 2, 0)), ((0, 0), (0, 0), (0, TEXT_PAD - TEXT))
    )
    first, text_keys, text_values = link([first, text_keys, text_values], [])
    own_weights = jnp.stack(
        [
            lax.dynamic_index_in_dim(w_o, expert, 0, False),
            jnp.swapaxes(lax.dynamic_index_in_dim(w_cq, expert, 0, False), 0, 1),
            lax.dynamic_index_in_dim(w_co, expert, 0, False),
        ]
    )
    heads_out, chunks = self_attend(
        normed, w_mixed, ([], [first, text_keys, text_values, own_weights, w_mixed])
    )
    all_weights = lax.all_gather(
        link([own_weights], [chunks[0][0]])[0], "tok", axis=0, tiled=False
    )

    def returned(value):
        back = lax.all_to_all(value, "tok", split_axis=0, concat_axis=0, tiled=True)
        return back.reshape(width, -1)

    turned = [returned(heads_out[0])]
    turned.append(returned(link([heads_out[1]], [turned[0], all_weights])[0]))
    predicted = finish(turned, latent, modulate[2][None], all_weights, text_keys, text_values)
    coefs = jnp.take(coef, lax.dynamic_slice_in_dim(timesteps, offset[0], steps))
    return over_steps(scan(coefs, first, over_steps(predicted))).reshape(1, count, width)


def solution(mesh):
    in_specs = (
        P("step", "tok", None),
        P(),
        P(),
        P(),
        P(),
        P(),
        P(None, None, "tok", None),
        P(None, "tok", None),
        P(None, None, "tok"),
        P(None, "tok", None),
        P(),
    )
    out_specs = P("step", "tok", None)
    return jax.shard_map(body, mesh=mesh, in_specs=in_specs, out_specs=out_specs, check_vma=False)
```

```python
import functools
import math

import jax
import jax.numpy as jnp
from jax import lax
from jax.experimental import pallas as pl
from jax.experimental.pallas import tpu as pltpu
from jax.sharding import PartitionSpec as P

HEAD = 72
LANES = 128
TEXT = 300
TEXT_PAD = 384
CHUNKS = (384, 128)
SOURCES = (4, 8)
ROW_BLOCK = 1024
ROWS = 128
KEY_BLOCK = 1024
HALVES = 2
VALUE = 2 * HEAD - LANES
FACTOR = math.log2(math.e) / HEAD**0.5
VMEM_LIMIT = 60 * 2**20
def link_kernel(passed, *refs):
    del passed, refs


def link(values, after):
    values = list(values)
    return pl.pallas_call(
        functools.partial(link_kernel, len(values)),
        in_specs=[pl.BlockSpec(memory_space=pl.ANY)] * (len(values) + len(after)),
        out_specs=[pl.BlockSpec(memory_space=pl.ANY)] * len(values),
        out_shape=[jax.ShapeDtypeStruct(value.shape, value.dtype) for value in values],
        input_output_aliases={index: index for index in range(len(values))},
        compiler_params=pltpu.CompilerParams(vmem_limit_bytes=VMEM_LIMIT),
        name="link",
    )(*values, *after)


def whole(array):
    return pl.BlockSpec(array.shape, lambda *_: (0,) * len(array.shape))


def norm_kernel(entry, latent, modulation, *outs):
    flat = latent[...].astype(jnp.float32)
    mean = jnp.mean(flat, axis=1, keepdims=True)
    centred = flat - mean
    var = jnp.mean(centred**2, axis=1, keepdims=True)
    row = pl.ds(entry[0] % 8, 1)
    shift, scale = modulation[0, row, :], modulation[1, row, :]
    normed = (centred * lax.rsqrt(var + 1e-06) * (1.0 + scale) + shift).astype(jnp.bfloat16)
    here = pl.program_id(0)
    first = CHUNKS[0] // ROWS

    @pl.when(here < first)
    def _():
        outs[0][...] = normed

    @pl.when(here >= first)
    def _():
        outs[1][...] = normed


def norm(latent, modulation, entry):
    count, width = latent.shape
    first = CHUNKS[0] // ROWS
    block = (ROWS, width)
    return pl.pallas_call(
        norm_kernel,
        grid_spec=pltpu.PrefetchScalarGridSpec(
            num_scalar_prefetch=1,
            grid=(count // ROWS,),
            in_specs=[
                pl.BlockSpec(block, lambda i, entry: (i, 0)),
                pl.BlockSpec((3, 8, width), lambda i, entry: (0, entry[0] // 8, 0)),
            ],
            out_specs=[
                pl.BlockSpec(block, lambda i, entry: (jnp.minimum(i, first - 1), 0)),
                pl.BlockSpec(block, lambda i, entry: (jnp.maximum(i - first, 0), 0)),
            ],
        ),
        out_shape=[jax.ShapeDtypeStruct((per, width), jnp.bfloat16) for per in CHUNKS],
        compiler_params=pltpu.CompilerParams(vmem_limit_bytes=VMEM_LIMIT),
        name="norm",
    )(entry, latent, modulation)


def project_kernel(waited, *refs):
    rows, weights, queries, keys, values = refs[waited:]
    mixed = jnp.dot(rows[...], weights[...], preferred_element_type=jnp.float32)
    low, high = mixed[:, :LANES], mixed[:, LANES:]
    queries[...] = low.astype(jnp.bfloat16)
    lane = lax.broadcasted_iota(jnp.int32, high.shape, 1)
    values[...] = jnp.where(lane >= VALUE + HEAD, 1.0, high).astype(jnp.bfloat16)
    pad = jnp.zeros((LANES - HEAD, mixed.shape[0]), jnp.float32)
    keys[...] = jnp.concatenate([low.T[HEAD:], high.T[:VALUE], pad], 0).astype(jnp.bfloat16)


def project(tokens, weights, after):
    count, width = tokens.shape
    flat = jax.ShapeDtypeStruct((count, LANES), jnp.bfloat16)
    turned = jax.ShapeDtypeStruct((LANES, count), jnp.bfloat16)
    flat_spec = pl.BlockSpec((ROW_BLOCK, LANES), lambda i: (i, 0))
    return pl.pallas_call(
        functools.partial(project_kernel, len(after)),
        grid=(count // ROW_BLOCK,),
        in_specs=[pl.BlockSpec(memory_space=pl.ANY)] * len(after)
        + [pl.BlockSpec((ROW_BLOCK, width), lambda i: (i, 0)), whole(weights)],
        out_specs=[flat_spec, pl.BlockSpec((LANES, ROW_BLOCK), lambda i: (0, i)), flat_spec],
        out_shape=(flat, turned, flat),
        compiler_params=pltpu.CompilerParams(vmem_limit_bytes=VMEM_LIMIT),
        cost_estimate=pl.CostEstimate(
            flops=4 * count * width * LANES,
            bytes_accessed=count * width * 2 + count * 6 * LANES,
            transcendentals=0,
        ),
        name="project",
    )(*after, tokens, weights)


def attend_kernel(waited, key_chunks, carried, final, *refs):
    refs = list(refs)[waited:]
    query_ref = refs.pop(0)
    keys = refs[:key_chunks]
    values = refs[key_chunks : 2 * key_chunks]
    del refs[: 2 * key_chunks]
    state = refs.pop(0) if carried else None
    out, scores = refs
    parts = [
        (key, value, slice(start, start + KEY_BLOCK))
        for key, value in zip(keys, values)
        for start in range(0, key.shape[1], KEY_BLOCK)
    ]
    rows = query_ref.shape[0] // HALVES
    spans = [slice(half * rows, (half + 1) * rows) for half in range(HALVES)]
    units = [(half, step) for step in range(len(parts)) for half in range(HALVES)]

    def score(unit):
        half, step = unit
        key, _, span = parts[step]
        return jnp.dot(
            query_ref[spans[half], :], key[:, span], preferred_element_type=jnp.float32
        )

    totals = [state[span, :] if carried else None for span in spans]
    tops = [total[:, LANES - 1 :] if carried else None for total in totals]
    scores[0] = score(units[0])
    for index, (half, step) in enumerate(units):
        if index + 1 < len(units):
            scores[(index + 1) % 2] = score(units[index + 1])
        now = scores[index % 2]
        top, total = tops[half], totals[half]
        high = jnp.max(now, axis=1, keepdims=True)
        newer = high if top is None else jnp.maximum(top, high)
        weights = jnp.exp2(now * FACTOR - newer * FACTOR).astype(jnp.bfloat16)
        _, value, span = parts[step]
        part = jnp.dot(weights, value[span, :], preferred_element_type=jnp.float32)
        totals[half] = part if top is None else total * jnp.exp2((top - newer) * FACTOR) + part
        tops[half] = newer
    for half, (total, top) in enumerate(zip(totals, tops)):
        if final:
            turned = total.T
            done = turned[VALUE : VALUE + HEAD] / turned[VALUE + HEAD : VALUE + HEAD + 1]
            per = out.shape[2]
            for piece in range(rows // per):
                out[half * (rows // per) + piece] = done[
                    :, piece * per : (piece + 1) * per
                ].astype(jnp.bfloat16)
        else:
            lane = lax.broadcasted_iota(jnp.int32, total.shape, 1)
            out[spans[half], :] = jnp.where(lane == LANES - 1, top, total)


def attend_chunk(queries, per, together, sources, state, final, after):
    count = queries.shape[0]
    block = per * together
    row_spec = pl.BlockSpec((block, LANES), lambda i: (i, 0))
    args = [*after, queries]
    in_specs = [pl.BlockSpec(memory_space=pl.ANY)] * len(after) + [row_spec]
    for index in (1, 2):
        args += [chunk[index] for chunk in sources]
        in_specs += [whole(chunk[index]) for chunk in sources]
    if state is not None:
        args.append(state)
        in_specs.append(row_spec)
    if final:
        out_shape = jax.ShapeDtypeStruct((count // per, HEAD, per), jnp.bfloat16)
        out_spec = pl.BlockSpec((together, HEAD, per), lambda i: (i, 0, 0))
    else:
        out_shape = jax.ShapeDtypeStruct((count, LANES), jnp.float32)
        out_spec = row_spec
    pairs = count * sum(chunk[1].shape[1] for chunk in sources)
    return pl.pallas_call(
        functools.partial(attend_kernel, len(after), len(sources), state is not None, final),
        grid=(count // block,),
        in_specs=in_specs,
        out_specs=out_spec,
        scratch_shapes=[
            pltpu.VMEM((2, block // HALVES, KEY_BLOCK), jnp.float32),
        ],
        out_shape=out_shape,
        compiler_params=pltpu.CompilerParams(vmem_limit_bytes=VMEM_LIMIT),
        cost_estimate=pl.CostEstimate(
            flops=4 * pairs * LANES * 2, bytes_accessed=4 * 2**20, transcendentals=pairs
        ),
        name="self_attend",
    )(*args)


def self_attend(normed, weights, early):
    chunks, states, previous = [], [], []
    held = None
    for chunk in range(len(CHUNKS)):
        own = normed[chunk]
        if held is not None:
            own = link([own], [held] + early[chunk])[0]
        held = lax.all_gather(own, "tok", axis=0, tiled=True)
        chunks.append([held])
    for chunk in range(len(CHUNKS)):
        last = chunk + 1 == len(CHUNKS)
        chunks[chunk] = project(chunks[chunk][0], weights, previous)
        for earlier in range(chunk + 1):
            before = states[earlier] if earlier < chunk else None
            keys = chunks[chunk : chunk + 1] if earlier < chunk else chunks[: chunk + 1]
            result = attend_chunk(
                chunks[earlier][0], CHUNKS[earlier], SOURCES[earlier], keys, before, last, previous
            )
            previous = [result]
            states[earlier : earlier + 1] = [result]
    return states, chunks


def finish_kernel(parts, *refs):
    turned, (latent, mix, weights, keys, values) = refs[:parts], refs[parts : parts + 5]
    out, cross, near, arrived = refs[parts + 5 :]
    width = latent.shape[1]
    copies = [
        pltpu.make_async_copy(weights.at[:, index], near.at[index], arrived.at[index])
        for index in range(3)
    ]
    for copy in copies:
        copy.start()

    def weight(index):
        copies[index].wait()
        return near[index].astype(jnp.float32).reshape(width, width).astype(jnp.bfloat16)

    attended = jnp.concatenate([part[...].astype(jnp.float32) for part in turned], 1)
    attended = attended.T.astype(jnp.bfloat16)
    projected = jnp.dot(attended, weight(0), preferred_element_type=jnp.float32)
    hidden = (latent[...].astype(jnp.float32) + mix[:1, :] * projected).astype(jnp.bfloat16)
    queries = lax.dot_general(
        weight(1), hidden, (((1,), (1,)), ((), ())), preferred_element_type=jnp.float32
    )
    for head in range(width // HEAD):
        rows = slice(head * HEAD, (head + 1) * HEAD)
        scores = jnp.dot(
            keys[head], queries[rows].astype(jnp.bfloat16), preferred_element_type=jnp.float32
        )
        row = lax.broadcasted_iota(jnp.int32, scores.shape, 0)
        scores = jnp.where(row < TEXT, scores, -jnp.inf)
        high = jnp.max(scores, axis=0, keepdims=True)
        exps = jnp.exp2((scores - high) * FACTOR)
        total = jnp.sum(exps, axis=0, keepdims=True)
        result = jnp.dot(
            values[head], exps.astype(jnp.bfloat16), preferred_element_type=jnp.float32
        )
        cross[rows, :] = result / total
    crossed = cross[...].T.astype(jnp.bfloat16)
    predicted = (
        hidden.astype(jnp.float32)
        + jnp.dot(crossed, weight(2), preferred_element_type=jnp.float32)
    ).astype(jnp.bfloat16)
    out[...] = (
        mix[1:2, :] * latent[...].astype(jnp.float32)
        + mix[2:3, :] * predicted.astype(jnp.float32)
    ).astype(jnp.bfloat16)


def finish(turned, latent, mix, weights, keys, values):
    count, width = latent.shape
    heads = width // HEAD
    args = (*turned, latent, mix, weights, keys, values)
    return pl.pallas_call(
        functools.partial(finish_kernel, len(turned)),
        grid=(1,),
        in_specs=[
            pl.BlockSpec(memory_space=pl.ANY) if arg is weights else whole(arg) for arg in args
        ],
        out_specs=whole(latent),
        out_shape=jax.ShapeDtypeStruct((count, width), jnp.bfloat16),
        scratch_shapes=[
            pltpu.VMEM((width, count), jnp.float32),
            pltpu.VMEM((3, heads, HEAD, width), jnp.bfloat16),
            pltpu.SemaphoreType.DMA((3,)),
        ],
        compiler_params=pltpu.CompilerParams(vmem_limit_bytes=VMEM_LIMIT),
        cost_estimate=pl.CostEstimate(
            flops=10 * count * width * width, bytes_accessed=10 * 2**20, transcendentals=0
        ),
        name="finish",
    )(*args)


def scan_kernel(coefs, everyone, out):
    out[0] = everyone[0]
    running = everyone[0].astype(jnp.float32)
    for step in range(1, everyone.shape[0]):
        running = running + coefs[step] * everyone[step].astype(jnp.float32)
        out[step] = running.astype(jnp.bfloat16)


def scan(coefs, everyone):
    return pl.pallas_call(
        scan_kernel,
        grid_spec=pltpu.PrefetchScalarGridSpec(
            num_scalar_prefetch=1,
            grid=(),
            in_specs=[pl.BlockSpec(memory_space=pltpu.VMEM)],
            out_specs=pl.BlockSpec(memory_space=pltpu.VMEM),
        ),
        out_shape=jax.ShapeDtypeStruct(everyone.shape, jnp.bfloat16),
        compiler_params=pltpu.CompilerParams(vmem_limit_bytes=16 * 2**20),
        name="scan",
    )(coefs, everyone)


def body(latents, timesteps, experts, offset, modulation, coef, w_qkv, w_o, w_cq, w_co, text_kv):
    step_index = lax.axis_index("step")
    steps = lax.axis_size("step")
    position = offset[0] + step_index
    entry = lax.dynamic_index_in_dim(timesteps, position, 0, False)
    expert = lax.dynamic_index_in_dim(experts, position, 0, False)
    modulate = lax.dynamic_index_in_dim(modulation, entry, 0, False)
    latent = latents[0]
    count, width = latent.shape
    heads = width // HEAD
    normed = norm(latent, jnp.swapaxes(modulation, 0, 1), entry[None])
    own_qkv = lax.dynamic_index_in_dim(w_qkv, expert, 0, False)[:, 0, :]
    w_mixed = jnp.pad(own_qkv, ((0, 0), (0, 2 * LANES - 3 * HEAD)))

    def over_steps(value):
        shaped = value.reshape(steps, -1, width)
        return lax.all_to_all(shaped, "step", split_axis=0, concat_axis=0, tiled=True)

    own_text = lax.dynamic_index_in_dim(text_kv, expert, 0, False).reshape(2, TEXT, heads, HEAD)
    text_keys = jnp.pad(
        jnp.transpose(own_text[0], (1, 0, 2)), ((0, 0), (0, TEXT_PAD - TEXT), (0, 0))
    )
    text_values = jnp.pad(
        jnp.transpose(own_text[1], (1, 2, 0)), ((0, 0), (0, 0), (0, TEXT_PAD - TEXT))
    )
    text_keys, text_values = link([text_keys, text_values], [])
    own_weights = jnp.stack(
        [
            lax.dynamic_index_in_dim(w_o, expert, 0, False),
            jnp.swapaxes(lax.dynamic_index_in_dim(w_cq, expert, 0, False), 0, 1),
            lax.dynamic_index_in_dim(w_co, expert, 0, False),
        ]
    )
    coefs = jnp.take(coef, lax.dynamic_slice_in_dim(timesteps, offset[0], steps))
    leads = step_index == 0
    mix = jnp.stack(
        [
            modulate[2],
            jnp.full((width,), jnp.where(leads, 1.0, 0.0)),
            jnp.full((width,), jnp.where(leads, coefs[0], 1.0)),
        ]
    )
    heads_out, chunks = self_attend(
        normed, w_mixed, ([], [text_keys, text_values, own_weights, w_mixed, mix])
    )
    all_weights = lax.all_gather(
        link([own_weights], [chunks[0][0]])[0], "tok", axis=0, tiled=False
    )

    def returned(value):
        back = lax.all_to_all(value, "tok", split_axis=0, concat_axis=0, tiled=True)
        return back.reshape(width, -1)

    turned = [returned(heads_out[0])]
    turned.append(returned(link([heads_out[1]], [turned[0], all_weights])[0]))
    sent = finish(turned, latent, mix, all_weights, text_keys, text_values)
    return over_steps(scan(coefs, over_steps(sent))).reshape(1, count, width)


def solution(mesh):
    in_specs = (
        P("step", "tok", None),
        P(),
        P(),
        P(),
        P(),
        P(),
        P(None, None, "tok", None),
        P(None, "tok", None),
        P(None, None, "tok"),
        P(None, "tok", None),
        P(),
    )
    out_specs = P("step", "tok", None)
    return jax.shard_map(body, mesh=mesh, in_specs=in_specs, out_specs=out_specs, check_vma=False)
```

```python
import functools
import math

import jax
import jax.numpy as jnp
from jax import lax
from jax.experimental import pallas as pl
from jax.experimental.pallas import tpu as pltpu
from jax.sharding import PartitionSpec as P

HEAD = 72
LANES = 128
TEXT = 300
TEXT_PAD = 384
CHUNKS = (384, 128)
SOURCES = (2, 8)
ROW_BLOCK = 1024
ROWS = 128
KEY_BLOCK = 1024
HALVES = 2
VALUE = 2 * HEAD - LANES
FACTOR = math.log2(math.e) / HEAD**0.5
VMEM_LIMIT = 60 * 2**20
def link_kernel(passed, *refs):
    del passed, refs


def link(values, after):
    values = list(values)
    return pl.pallas_call(
        functools.partial(link_kernel, len(values)),
        in_specs=[pl.BlockSpec(memory_space=pl.ANY)] * (len(values) + len(after)),
        out_specs=[pl.BlockSpec(memory_space=pl.ANY)] * len(values),
        out_shape=[jax.ShapeDtypeStruct(value.shape, value.dtype) for value in values],
        input_output_aliases={index: index for index in range(len(values))},
        compiler_params=pltpu.CompilerParams(vmem_limit_bytes=VMEM_LIMIT),
        name="link",
    )(*values, *after)


def whole(array):
    return pl.BlockSpec(array.shape, lambda *_: (0,) * len(array.shape))


def norm_kernel(entry, latent, modulation, *outs):
    flat = latent[...].astype(jnp.float32)
    mean = jnp.mean(flat, axis=1, keepdims=True)
    centred = flat - mean
    var = jnp.mean(centred**2, axis=1, keepdims=True)
    row = pl.ds(entry[0] % 8, 1)
    shift, scale = modulation[0, row, :], modulation[1, row, :]
    normed = (centred * lax.rsqrt(var + 1e-06) * (1.0 + scale) + shift).astype(jnp.bfloat16)
    here = pl.program_id(0)
    first = CHUNKS[0] // ROWS

    @pl.when(here < first)
    def _():
        outs[0][...] = normed

    @pl.when(here >= first)
    def _():
        outs[1][...] = normed


def norm(latent, modulation, entry):
    count, width = latent.shape
    first = CHUNKS[0] // ROWS
    block = (ROWS, width)
    return pl.pallas_call(
        norm_kernel,
        grid_spec=pltpu.PrefetchScalarGridSpec(
            num_scalar_prefetch=1,
            grid=(count // ROWS,),
            in_specs=[
                pl.BlockSpec(block, lambda i, entry: (i, 0)),
                pl.BlockSpec((3, 8, width), lambda i, entry: (0, entry[0] // 8, 0)),
            ],
            out_specs=[
                pl.BlockSpec(block, lambda i, entry: (jnp.minimum(i, first - 1), 0)),
                pl.BlockSpec(block, lambda i, entry: (jnp.maximum(i - first, 0), 0)),
            ],
        ),
        out_shape=[jax.ShapeDtypeStruct((per, width), jnp.bfloat16) for per in CHUNKS],
        compiler_params=pltpu.CompilerParams(vmem_limit_bytes=VMEM_LIMIT),
        name="norm",
    )(entry, latent, modulation)


def project_kernel(waited, *refs):
    rows, weights, queries, keys, values = refs[waited:]
    mixed = jnp.dot(rows[...], weights[...], preferred_element_type=jnp.float32)
    low, high = mixed[:, :LANES], mixed[:, LANES:]
    queries[...] = low.astype(jnp.bfloat16)
    lane = lax.broadcasted_iota(jnp.int32, high.shape, 1)
    values[...] = jnp.where(lane >= VALUE + HEAD, 1.0, high).astype(jnp.bfloat16)
    pad = jnp.zeros((LANES - HEAD, mixed.shape[0]), jnp.float32)
    keys[...] = jnp.concatenate([low.T[HEAD:], high.T[:VALUE], pad], 0).astype(jnp.bfloat16)


def project(tokens, weights, after):
    count, width = tokens.shape
    flat = jax.ShapeDtypeStruct((count, LANES), jnp.bfloat16)
    turned = jax.ShapeDtypeStruct((LANES, count), jnp.bfloat16)
    flat_spec = pl.BlockSpec((ROW_BLOCK, LANES), lambda i: (i, 0))
    return pl.pallas_call(
        functools.partial(project_kernel, len(after)),
        grid=(count // ROW_BLOCK,),
        in_specs=[pl.BlockSpec(memory_space=pl.ANY)] * len(after)
        + [pl.BlockSpec((ROW_BLOCK, width), lambda i: (i, 0)), whole(weights)],
        out_specs=[flat_spec, pl.BlockSpec((LANES, ROW_BLOCK), lambda i: (0, i)), flat_spec],
        out_shape=(flat, turned, flat),
        compiler_params=pltpu.CompilerParams(vmem_limit_bytes=VMEM_LIMIT),
        cost_estimate=pl.CostEstimate(
            flops=4 * count * width * LANES,
            bytes_accessed=count * width * 2 + count * 6 * LANES,
            transcendentals=0,
        ),
        name="project",
    )(*after, tokens, weights)


def attend_kernel(waited, key_chunks, carried, final, *refs):
    refs = list(refs)[waited:]
    query_ref = refs.pop(0)
    keys = refs[:key_chunks]
    values = refs[key_chunks : 2 * key_chunks]
    del refs[: 2 * key_chunks]
    state = refs.pop(0) if carried else None
    out, scores = refs
    parts = [
        (key, value, slice(start, start + KEY_BLOCK))
        for key, value in zip(keys, values)
        for start in range(0, key.shape[1], KEY_BLOCK)
    ]
    rows = query_ref.shape[0] // HALVES
    spans = [slice(half * rows, (half + 1) * rows) for half in range(HALVES)]
    units = [(half, step) for step in range(len(parts)) for half in range(HALVES)]

    def score(unit):
        half, step = unit
        key, _, span = parts[step]
        return jnp.dot(
            query_ref[spans[half], :], key[:, span], preferred_element_type=jnp.float32
        )

    totals = [state[span, :] if carried else None for span in spans]
    tops = [total[:, LANES - 1 :] if carried else None for total in totals]
    scores[0] = score(units[0])
    for index, (half, step) in enumerate(units):
        if index + 1 < len(units):
            scores[(index + 1) % 2] = score(units[index + 1])
        now = scores[index % 2]
        top, total = tops[half], totals[half]
        high = jnp.max(now, axis=1, keepdims=True)
        newer = high if top is None else jnp.maximum(top, high)
        weights = jnp.exp2(now * FACTOR - newer * FACTOR).astype(jnp.bfloat16)
        _, value, span = parts[step]
        part = jnp.dot(weights, value[span, :], preferred_element_type=jnp.float32)
        totals[half] = part if top is None else total * jnp.exp2((top - newer) * FACTOR) + part
        tops[half] = newer
    for half, (total, top) in enumerate(zip(totals, tops)):
        if final:
            turned = total.T
            done = turned[VALUE : VALUE + HEAD] / turned[VALUE + HEAD : VALUE + HEAD + 1]
            per = out.shape[2]
            for piece in range(rows // per):
                out[half * (rows // per) + piece] = done[
                    :, piece * per : (piece + 1) * per
                ].astype(jnp.bfloat16)
        else:
            lane = lax.broadcasted_iota(jnp.int32, total.shape, 1)
            out[spans[half], :] = jnp.where(lane == LANES - 1, top, total)


def attend_chunk(queries, per, together, sources, state, final, after):
    count = queries.shape[0]
    block = per * together
    row_spec = pl.BlockSpec((block, LANES), lambda i: (i, 0))
    args = [*after, queries]
    in_specs = [pl.BlockSpec(memory_space=pl.ANY)] * len(after) + [row_spec]
    for index in (1, 2):
        args += [chunk[index] for chunk in sources]
        in_specs += [whole(chunk[index]) for chunk in sources]
    if state is not None:
        args.append(state)
        in_specs.append(row_spec)
    if final:
        out_shape = jax.ShapeDtypeStruct((count // per, HEAD, per), jnp.bfloat16)
        out_spec = pl.BlockSpec((together, HEAD, per), lambda i: (i, 0, 0))
    else:
        out_shape = jax.ShapeDtypeStruct((count, LANES), jnp.float32)
        out_spec = row_spec
    pairs = count * sum(chunk[1].shape[1] for chunk in sources)
    return pl.pallas_call(
        functools.partial(attend_kernel, len(after), len(sources), state is not None, final),
        grid=(count // block,),
        in_specs=in_specs,
        out_specs=out_spec,
        scratch_shapes=[
            pltpu.VMEM((2, block // HALVES, KEY_BLOCK), jnp.float32),
        ],
        out_shape=out_shape,
        compiler_params=pltpu.CompilerParams(vmem_limit_bytes=VMEM_LIMIT),
        cost_estimate=pl.CostEstimate(
            flops=4 * pairs * LANES * 2, bytes_accessed=4 * 2**20, transcendentals=pairs
        ),
        name="self_attend",
    )(*args)


def self_attend(normed, weights, early):
    chunks, states, previous = [], [], []
    held = None
    for chunk in range(len(CHUNKS)):
        own = normed[chunk]
        if held is not None:
            own = link([own], [held] + early[chunk])[0]
        held = lax.all_gather(own, "tok", axis=0, tiled=True)
        chunks.append([held])
    for chunk in range(len(CHUNKS)):
        last = chunk + 1 == len(CHUNKS)
        chunks[chunk] = project(chunks[chunk][0], weights, previous)
        for earlier in range(chunk + 1):
            before = states[earlier] if earlier < chunk else None
            keys = chunks[chunk : chunk + 1] if earlier < chunk else chunks[: chunk + 1]
            result = attend_chunk(
                chunks[earlier][0],
                CHUNKS[earlier],
                SOURCES[earlier] * (2 if earlier < chunk else 1),
                keys,
                before,
                last,
                previous,
            )
            previous = [result]
            states[earlier : earlier + 1] = [result]
    return states, chunks


def finish_kernel(parts, *refs):
    turned, (latent, mix, weights, keys, values) = refs[:parts], refs[parts : parts + 5]
    out, cross, near, arrived = refs[parts + 5 :]
    width = latent.shape[1]
    copies = [
        pltpu.make_async_copy(weights.at[:, index], near.at[index], arrived.at[index])
        for index in range(3)
    ]
    for copy in copies:
        copy.start()

    def weight(index):
        copies[index].wait()
        return near[index].astype(jnp.float32).reshape(width, width).astype(jnp.bfloat16)

    attended = jnp.concatenate([part[...].astype(jnp.float32) for part in turned], 1)
    attended = attended.T.astype(jnp.bfloat16)
    projected = jnp.dot(attended, weight(0), preferred_element_type=jnp.float32)
    hidden = (latent[...].astype(jnp.float32) + mix[:1, :] * projected).astype(jnp.bfloat16)
    queries = lax.dot_general(
        weight(1), hidden, (((1,), (1,)), ((), ())), preferred_element_type=jnp.float32
    )
    for head in range(width // HEAD):
        rows = slice(head * HEAD, (head + 1) * HEAD)
        scores = jnp.dot(
            keys[head], queries[rows].astype(jnp.bfloat16), preferred_element_type=jnp.float32
        )
        row = lax.broadcasted_iota(jnp.int32, scores.shape, 0)
        scores = jnp.where(row < TEXT, scores, -jnp.inf)
        high = jnp.max(scores, axis=0, keepdims=True)
        exps = jnp.exp2((scores - high) * FACTOR)
        total = jnp.sum(exps, axis=0, keepdims=True)
        result = jnp.dot(
            values[head], exps.astype(jnp.bfloat16), preferred_element_type=jnp.float32
        )
        cross[rows, :] = result / total
    crossed = cross[...].T.astype(jnp.bfloat16)
    predicted = (
        hidden.astype(jnp.float32)
        + jnp.dot(crossed, weight(2), preferred_element_type=jnp.float32)
    ).astype(jnp.bfloat16)
    out[...] = (
        mix[1:2, :] * latent[...].astype(jnp.float32)
        + mix[2:3, :] * predicted.astype(jnp.float32)
    ).astype(jnp.bfloat16)


def finish(turned, latent, mix, weights, keys, values):
    count, width = latent.shape
    heads = width // HEAD
    args = (*turned, latent, mix, weights, keys, values)
    return pl.pallas_call(
        functools.partial(finish_kernel, len(turned)),
        grid=(1,),
        in_specs=[
            pl.BlockSpec(memory_space=pl.ANY) if arg is weights else whole(arg) for arg in args
        ],
        out_specs=whole(latent),
        out_shape=jax.ShapeDtypeStruct((count, width), jnp.bfloat16),
        scratch_shapes=[
            pltpu.VMEM((width, count), jnp.float32),
            pltpu.VMEM((3, heads, HEAD, width), jnp.bfloat16),
            pltpu.SemaphoreType.DMA((3,)),
        ],
        compiler_params=pltpu.CompilerParams(vmem_limit_bytes=VMEM_LIMIT),
        cost_estimate=pl.CostEstimate(
            flops=10 * count * width * width, bytes_accessed=10 * 2**20, transcendentals=0
        ),
        name="finish",
    )(*args)


def scan_kernel(coefs, everyone, out):
    out[0] = everyone[0]
    running = everyone[0].astype(jnp.float32)
    for step in range(1, everyone.shape[0]):
        running = running + coefs[step] * everyone[step].astype(jnp.float32)
        out[step] = running.astype(jnp.bfloat16)


def scan(coefs, everyone):
    return pl.pallas_call(
        scan_kernel,
        grid_spec=pltpu.PrefetchScalarGridSpec(
            num_scalar_prefetch=1,
            grid=(),
            in_specs=[pl.BlockSpec(memory_space=pltpu.VMEM)],
            out_specs=pl.BlockSpec(memory_space=pltpu.VMEM),
        ),
        out_shape=jax.ShapeDtypeStruct(everyone.shape, jnp.bfloat16),
        compiler_params=pltpu.CompilerParams(vmem_limit_bytes=16 * 2**20),
        name="scan",
    )(coefs, everyone)


def body(latents, timesteps, experts, offset, modulation, coef, w_qkv, w_o, w_cq, w_co, text_kv):
    step_index = lax.axis_index("step")
    steps = lax.axis_size("step")
    position = offset[0] + step_index
    entry = lax.dynamic_index_in_dim(timesteps, position, 0, False)
    expert = lax.dynamic_index_in_dim(experts, position, 0, False)
    modulate = lax.dynamic_index_in_dim(modulation, entry, 0, False)
    latent = latents[0]
    count, width = latent.shape
    heads = width // HEAD
    normed = norm(latent, jnp.swapaxes(modulation, 0, 1), entry[None])
    own_qkv = lax.dynamic_index_in_dim(w_qkv, expert, 0, False)[:, 0, :]
    w_mixed = jnp.pad(own_qkv, ((0, 0), (0, 2 * LANES - 3 * HEAD)))

    def over_steps(value):
        shaped = value.reshape(steps, -1, width)
        return lax.all_to_all(shaped, "step", split_axis=0, concat_axis=0, tiled=True)

    own_text = lax.dynamic_index_in_dim(text_kv, expert, 0, False).reshape(2, TEXT, heads, HEAD)
    text_keys = jnp.pad(
        jnp.transpose(own_text[0], (1, 0, 2)), ((0, 0), (0, TEXT_PAD - TEXT), (0, 0))
    )
    text_values = jnp.pad(
        jnp.transpose(own_text[1], (1, 2, 0)), ((0, 0), (0, 0), (0, TEXT_PAD - TEXT))
    )
    text_keys, text_values = link([text_keys, text_values], [])
    own_weights = jnp.stack(
        [
            lax.dynamic_index_in_dim(w_o, expert, 0, False),
            jnp.swapaxes(lax.dynamic_index_in_dim(w_cq, expert, 0, False), 0, 1),
            lax.dynamic_index_in_dim(w_co, expert, 0, False),
        ]
    )
    coefs = jnp.take(coef, lax.dynamic_slice_in_dim(timesteps, offset[0], steps))
    leads = step_index == 0
    mix = jnp.stack(
        [
            modulate[2],
            jnp.full((width,), jnp.where(leads, 1.0, 0.0)),
            jnp.full((width,), jnp.where(leads, coefs[0], 1.0)),
        ]
    )
    heads_out, chunks = self_attend(
        normed, w_mixed, ([], [text_keys, text_values, own_weights, w_mixed, mix])
    )
    all_weights = lax.all_gather(
        link([own_weights], [chunks[0][0]])[0], "tok", axis=0, tiled=False
    )

    def returned(value):
        back = lax.all_to_all(value, "tok", split_axis=0, concat_axis=0, tiled=True)
        return back.reshape(width, -1)

    turned = [returned(heads_out[0])]
    turned.append(returned(link([heads_out[1]], [turned[0], all_weights])[0]))
    sent = [
        finish([part], rows, mix, all_weights, text_keys, text_values)
        for part, rows in zip(turned, jnp.split(latent, [CHUNKS[0]]))
    ]
    return over_steps(scan(coefs, over_steps(jnp.concatenate(sent, 0)))).reshape(1, count, width)


def solution(mesh):
    in_specs = (
        P("step", "tok", None),
        P(),
        P(),
        P(),
        P(),
        P(),
        P(None, None, "tok", None),
        P(None, "tok", None),
        P(None, None, "tok"),
        P(None, "tok", None),
        P(),
    )
    out_specs = P("step", "tok", None)
    return jax.shard_map(body, mesh=mesh, in_specs=in_specs, out_specs=out_specs, check_vma=False)
```
